512 devices in a mesh: dp: 32 (over z, x), seq: 16 (over y, core).
Axes of the slice: x: 4, y: 8, z: 8, core: 2. Of those that a mesh axis runs over, the one named last changes fastest.
Arguments:
- features: bfloat16 [32, 3584, 1024], P('dp', 'seq'), may hold values from -6 to 6
- queries: bfloat16 [32, 3584, 1024], P('dp', 'seq'), may hold values from -4.5 to 4.5
- key_rows: bfloat16 [32, 3584, 1024], P('dp', 'seq'), may hold values from -4.5 to 4.5
- kernel: float32 [9, 1024], replicated, may hold values from -1.5 to 1.5
- out_weight: bfloat16 [1024, 1024], P(None, 'seq'), may hold values from -0.1875 to 0.1875
- cotangent: bfloat16 [32, 3584, 1024], P('dp', 'seq'), may hold values from -6 to 6
- lengths: int32 [32, 16], P('dp'), may hold values from 1 to 672, 3584 in all within a row
Outputs:
- layer_out: bfloat16 [32, 3584, 1024], P('dp', 'seq')
- grad_queries: bfloat16 [32, 3584, 1024], P('dp', 'seq')
- grad_keys: bfloat16 [32, 3584, 1024], P('dp', 'seq')
- grad_features: bfloat16 [32, 3584, 1024], P('dp', 'seq')
- grad_kernel: float32 [9, 1024], replicated
- grad_out_weight: float32 [1024, 1024], P(('dp', 'seq'))
The draws below stay inside these ranges and needn't reach their ends.
Inputs may be any that keep to these rules, and one draw needn't show every extreme that they name: Each row holds 16 utterance lengths that sum to 3584.
All inputs are finite; a program needn't handle non-finite values.
Results may differ from the reference program's by a relative error of at most 0.012.
The reference program's roundings to bfloat16 on the way count: a program that leaves them out, or rounds other values in their place, can miss the bound.
Values may be sent and summed in bfloat16 or wider, within the bound.
A program may use at most 128 MiB of HBM per device.

```python
import math
import jax
import jax.numpy as jnp
import numpy as np
from jax import lax

D = 1024
HEADS = 8
SEQ_DEV = 224
HALF = 128
KERNEL = 9
UTT = 16
BATCH = 32
SEQLEN = 3584
N_SEQ = 16


def draw_queries(key, part):
    key = jax.random.fold_in(key, 11)
    values = jnp.clip(jax.random.normal(key, (BATCH, SEQLEN, D), jnp.float32), -4.5, 4.5)
    return values.astype(jnp.bfloat16)


def draw_key_rows(key, part):
    key = jax.random.fold_in(key, 23)
    values = jnp.clip(jax.random.normal(key, (BATCH, SEQLEN, D), jnp.float32), -4.5, 4.5)
    return values.astype(jnp.bfloat16)


def block_levels(stream_key, extent, cuts, least, largest):
    factor_of = 1.0
    for dim, parts in cuts:
        steps = jax.random.uniform(jax.random.fold_in(jax.random.fold_in(stream_key, 6), dim), (parts,), jnp.float32, least / len(cuts), largest / len(cuts))
        factor_of = factor_of * jnp.repeat(jnp.exp(steps), extent[dim] // parts).reshape((-1,) + (1,) * (len(extent) - 1 - dim))
    return factor_of


def length_profile(amount, total, bound, slope):
    loads = [(1 << 20) // math.isqrt(rank ** slope) + 1 for rank in range(2, amount + 1)]
    surplus, counts = total - bound - (amount - 1), [1] * (amount - 1)
    while surplus > 0:
        movable = [i for i in range(amount - 1) if counts[i] < bound]
        mass, budget = sum([loads[i] for i in movable]), surplus
        for i in movable:
            extra = min(bound - counts[i], max(1, budget * loads[i] // mass), surplus)
            counts[i] = counts[i] + extra
            surplus = surplus - extra
    return np.array([bound] + counts)


def ragged_sizes(key, amount, total, limit, slope):
    if amount == 2:
        one = jax.random.randint(key, (), max(1, total - limit), min(limit, total - 1) + 1)
        return jnp.stack([one, total - one])
    tallies = jnp.asarray(length_profile(amount, total, limit, slope), jnp.int32)
    pairs = (amount - 1) // 2
    donor, taker = tallies[1:1 + 2 * pairs:2], tallies[2:2 + 2 * pairs:2]
    room = jnp.minimum(donor - 1, limit - taker)
    moved = jax.random.randint(jax.random.fold_in(key, 1), (pairs,), 0, 1 << 20) % (room + 1)
    tallies = tallies.at[1:1 + 2 * pairs:2].set(donor - moved).at[2:2 + 2 * pairs:2].set(taker + moved)
    return tallies[jax.random.permutation(jax.random.fold_in(key, 2), amount)]


def noise(rng, extent, deviation, limit, cuts=(), kind=jnp.bfloat16):
    result = deviation * jax.random.normal(rng, extent, jnp.float32)
    if cuts:
        result = result * block_levels(rng, extent, cuts, -0.22, 0.18)
    return jnp.clip(result, -limit, limit).astype(kind)


def setup_inputs(seed: int = 0) -> dict:
    keys = jax.random.split(jax.random.key(seed), 8)
    return {
        "features": noise(keys[0], (BATCH, SEQLEN, D), 1.0, 6.0, ((0, 32), (1, 16))),
        "queries": draw_queries(jax.random.fold_in(keys[7], 71), 0),
        "key_rows": draw_key_rows(jax.random.fold_in(keys[7], 71), 0),
        "kernel": noise(keys[3], (KERNEL, D), 0.3, 1.5, (), jnp.float32),
        "out_weight": noise(keys[4], (D, D), D ** -0.5, 0.1875, ((1, 16),)),
        "cotangent": noise(keys[5], (BATCH, SEQLEN, D), 1.0, 6.0, ((0, 32), (1, 16))),
        "lengths": jax.vmap(lambda own: ragged_sizes(own, UTT, SEQLEN, 3 * SEQLEN // UTT, 2))(jax.random.split(keys[6], BATCH)).reshape((BATCH, UTT)).astype(jnp.int32),
    }


def to_float(rounded):
    return lax.optimization_barrier(rounded).astype(jnp.float32)


def segment_of(positions, bounds):
    return jnp.sum((positions[:, None] >= bounds[None, :]).astype(jnp.int32), axis=1)


def pair_mask(center_pos, source_pos, bounds, seqlen):
    valid_c = (center_pos >= 0) & (center_pos < seqlen)
    valid_s = (source_pos >= 0) & (source_pos < seqlen)
    return valid_c & valid_s & (segment_of(center_pos, bounds) == segment_of(source_pos, bounds))


def window_mask(query_pos, key_pos, bounds, seqlen):
    valid_q = (query_pos >= 0) & (query_pos < seqlen)
    valid_k = (key_pos >= 0) & (key_pos < seqlen)
    same = segment_of(query_pos, bounds)[:, None] == segment_of(key_pos, bounds)[None, :]
    near = jnp.abs(query_pos[:, None] - key_pos[None, :]) <= HALF
    return valid_q[:, None] & valid_k[None, :] & same & near


def depthwise(source, source_pos, kernel, row_count, bounds, seqlen):
    reach = (kernel.shape[0] - 1) // 2
    center = source_pos[reach:reach + row_count]
    running = jnp.zeros((row_count, source.shape[1]), jnp.float32)
    for tap_index in range(kernel.shape[0]):
        matches = pair_mask(center, source_pos[tap_index:tap_index + row_count], bounds, seqlen)
        term = kernel[tap_index][None, :] * source[tap_index:tap_index + row_count].astype(jnp.float32)
        running = running + jnp.where(matches[:, None], term, 0.0)
    return running


def conv_back(grad_rim, rim_pos, kernel, row_count, bounds, seqlen):
    reach = (kernel.shape[0] - 1) // 2
    center = rim_pos[reach:reach + row_count]
    running = jnp.zeros((row_count, grad_rim.shape[1]), jnp.float32)
    for tap_index in range(kernel.shape[0]):
        low = 2 * reach - tap_index
        matches = pair_mask(center, rim_pos[low:low + row_count], bounds, seqlen)
        term = kernel[tap_index][None, :] * grad_rim[low:low + row_count]
        running = running + jnp.where(matches[:, None], term, 0.0)
    return running


def kernel_terms(grad_values, input_rim, rim_pos, kernel, row_count, bounds, seqlen):
    reach = (kernel.shape[0] - 1) // 2
    center = rim_pos[reach:reach + row_count]
    rows_out = []
    for tap_index in range(kernel.shape[0]):
        matches = pair_mask(center, rim_pos[tap_index:tap_index + row_count], bounds, seqlen)
        term = grad_values * input_rim[tap_index:tap_index + row_count].astype(jnp.float32)
        rows_out.append(jnp.sum(jnp.where(matches[:, None], term, 0.0), axis=0))
    return jnp.stack(rows_out)


def head_inner(back, mixed):
    product = back.astype(jnp.float32) * mixed.astype(jnp.float32)
    return jnp.sum(product.reshape(product.shape[0], HEADS, -1), axis=2).T


def forward_attention(query_block, key_ext, value_ext, allowed):
    row_count = query_block.shape[0]
    query_h = query_block.astype(jnp.float32).reshape(row_count, HEADS, -1)
    key_h = key_ext.astype(jnp.float32).reshape(key_ext.shape[0], HEADS, -1)
    value_h = value_ext.astype(jnp.float32).reshape(value_ext.shape[0], HEADS, -1)
    score_scale = query_h.shape[-1] ** -0.5
    scores = jnp.einsum('thd,uhd->htu', query_h, key_h) * score_scale
    masked = jnp.where(allowed[None], scores, -jnp.inf)
    row_max = jnp.max(masked, axis=-1, keepdims=True)
    exponent = jnp.where(allowed[None], jnp.exp(masked - row_max), 0.0)
    sums = jnp.sum(exponent, axis=-1, keepdims=True)
    probs_bf = (exponent / sums).astype(jnp.bfloat16)
    mixed = jnp.einsum('htu,uhd->thd', to_float(probs_bf), value_h)
    log_total = (row_max + jnp.log(sums))[..., 0]
    return mixed.reshape(row_count, -1).astype(jnp.bfloat16), log_total


def backward_attention(query_block, key_ext, value_ext, back_block, inner, log_total, allowed):
    row_count = query_block.shape[0]
    query_h = query_block.astype(jnp.float32).reshape(row_count, HEADS, -1)
    back_h = back_block.astype(jnp.float32).reshape(row_count, HEADS, -1)
    key_h = key_ext.astype(jnp.float32).reshape(key_ext.shape[0], HEADS, -1)
    value_h = value_ext.astype(jnp.float32).reshape(value_ext.shape[0], HEADS, -1)
    score_scale = query_h.shape[-1] ** -0.5
    scores = jnp.einsum('thd,uhd->htu', query_h, key_h) * score_scale
    again = jnp.where(allowed[None], jnp.exp(jnp.where(allowed[None], scores, 0.0) - log_total[..., None]), 0.0)
    again_bf = again.astype(jnp.bfloat16)
    dprob = jnp.einsum('thd,uhd->htu', back_h, value_h)
    dscore = (again * (dprob - inner[..., None])).astype(jnp.bfloat16)
    grad_q = jnp.einsum('htu,uhd->thd', to_float(dscore), key_h) * score_scale
    grad_k = jnp.einsum('htu,thd->uhd', to_float(dscore), query_h) * score_scale
    grad_v = jnp.einsum('htu,thd->uhd', to_float(again_bf), back_h)
    return grad_q.reshape(row_count, -1), grad_k.reshape(key_ext.shape[0], -1), grad_v.reshape(key_ext.shape[0], -1)


def reference(features, queries, key_rows, kernel, out_weight, cotangent, lengths):
    reach = (kernel.shape[0] - 1) // 2
    margin = HALF + reach
    span = SEQ_DEV + 2 * HALF

    def one_row(row):
        inputs_row, query_row, key_row, cot_row, length_row = row
        bounds = jnp.cumsum(length_row).astype(jnp.int32)
        padded_in = jnp.pad(inputs_row, ((margin, margin), (0, 0)))
        padded_pos = jnp.arange(SEQLEN + 2 * margin, dtype=jnp.int32) - margin
        value_ext = depthwise(padded_in, padded_pos, kernel, SEQLEN + 2 * HALF, bounds, SEQLEN).astype(jnp.bfloat16)
        key_ext = jnp.pad(key_row, ((HALF, HALF), (0, 0)))

        def block_mask(block_index):
            begin = block_index * SEQ_DEV
            query_pos = begin + jnp.arange(SEQ_DEV, dtype=jnp.int32)
            key_pos = begin - HALF + jnp.arange(span, dtype=jnp.int32)
            return begin, window_mask(query_pos, key_pos, bounds, SEQLEN)

        def block_forward(block_index):
            begin, allowed = block_mask(block_index)
            query_block = lax.dynamic_slice_in_dim(query_row, begin, SEQ_DEV, 0)
            key_block = lax.dynamic_slice_in_dim(key_ext, begin, span, 0)
            value_block = lax.dynamic_slice_in_dim(value_ext, begin, span, 0)
            return forward_attention(query_block, key_block, value_block, allowed)

        mixed_blocks, log_blocks = lax.map(block_forward, jnp.arange(N_SEQ, dtype=jnp.int32))
        mixed = mixed_blocks.reshape(SEQLEN, D)
        layer = jnp.dot(mixed, out_weight, preferred_element_type=jnp.float32).astype(jnp.bfloat16)
        back = lax.dot_general(cot_row, out_weight, (((1,), (1,)), ((), ())), preferred_element_type=jnp.float32).astype(jnp.bfloat16)
        weight_part = lax.dot_general(mixed, cot_row, (((0,), (0,)), ((), ())), preferred_element_type=jnp.float32)
        inner = head_inner(back, mixed)

        def block_backward(carry, block_index):
            grad_k_pad, grad_v_pad = carry
            begin, allowed = block_mask(block_index)
            query_block = lax.dynamic_slice_in_dim(query_row, begin, SEQ_DEV, 0)
            back_block = lax.dynamic_slice_in_dim(back, begin, SEQ_DEV, 0)
            inner_block = lax.dynamic_slice_in_dim(inner, begin, SEQ_DEV, 1)
            key_block = lax.dynamic_slice_in_dim(key_ext, begin, span, 0)
            value_block = lax.dynamic_slice_in_dim(value_ext, begin, span, 0)
            grad_q, grad_k, grad_v = backward_attention(query_block, key_block, value_block, back_block, inner_block, log_blocks[block_index], allowed)
            grad_k_pad = lax.dynamic_update_slice_in_dim(grad_k_pad, lax.dynamic_slice_in_dim(grad_k_pad, begin, span, 0) + grad_k, begin, 0)
            grad_v_pad = lax.dynamic_update_slice_in_dim(grad_v_pad, lax.dynamic_slice_in_dim(grad_v_pad, begin, span, 0) + grad_v, begin, 0)
            return (grad_k_pad, grad_v_pad), grad_q

        zeros = jnp.zeros((SEQLEN + 2 * HALF, D), jnp.float32)
        (grad_k_pad, grad_v_pad), grad_q_blocks = lax.scan(block_backward, (zeros, zeros), jnp.arange(N_SEQ, dtype=jnp.int32))
        grad_values = grad_v_pad[HALF:HALF + SEQLEN]
        rim_pos = jnp.arange(SEQLEN + 2 * reach, dtype=jnp.int32) - reach
        grad_in = conv_back(jnp.pad(grad_values, ((reach, reach), (0, 0))), rim_pos, kernel, SEQLEN, bounds, SEQLEN)
        kernel_part = kernel_terms(grad_values, jnp.pad(inputs_row, ((reach, reach), (0, 0))), rim_pos, kernel, SEQLEN, bounds, SEQLEN)
        return (layer, grad_q_blocks.reshape(SEQLEN, D).astype(jnp.bfloat16), grad_k_pad[HALF:HALF + SEQLEN].astype(jnp.bfloat16),
                grad_in.astype(jnp.bfloat16), kernel_part, weight_part)

    layer_out, grad_queries, grad_keys, grad_features, kernel_parts, weight_parts = lax.map(
        one_row, (features, queries, key_rows, cotangent, lengths))
    norm = float(BATCH * SEQLEN) ** -0.5
    grad_kernel = jnp.sum(kernel_parts, axis=0) * norm
    grad_out_weight = jnp.sum(weight_parts, axis=0) * norm
    return layer_out, grad_queries, grad_keys, grad_features, grad_kernel, grad_out_weight
```

```python
import functools
import math

import jax
import jax.numpy as jnp
from jax import lax
from jax.experimental import pallas as pl
from jax.experimental.pallas import tpu as pltpu
from jax.sharding import PartitionSpec as P

MESH = pl.DeviceIdType.MESH
F32 = jnp.float32
BF16 = jnp.bfloat16

HALF = 128
TAPS = 9
REACH = 4
RIM = 16
UTT = 16
ROWS = 224
WIDTH = 1024
HEAD = 128
PAIR = 256
GROUPS = 4
NX = 4
NZ = 8
NY = 8
EXT = ROWS + 2 * HALF
FEXT = EXT + 2 * RIM
FHALO = HALF + RIM
BLK = 112
SPAN = 384
BLKOFF = 96
NSEM = 160


def dot(a, b, contract):
    return lax.dot_general(a, b, ((contract[:1], contract[1:]), ((), ())), preferred_element_type=F32)


def kernel(
    norm,
    feat, qry, key, ker, wgt, cot, lens,
    o_layer, o_gq, o_gk, o_gf, o_gker, o_gw,
    fext, fs, kext, qv, cotv, kerv, segs, taps, bias, vext, probs, mixed,
    wown, wsib, wpiece, wblk, wfull,
    gsend, gown, gcore, gx, gxr, gz, gzr, gs, gsr, gwv,
    dqv, dkx, dvx, dks, dvs, dkr, dvr, dkv, gfv, lay,
    kp, kpr, kz, kzr, ky, kyr, kfin, kall, kout,
    ss, rs, ls,
):
    dp = lax.axis_index("dp")
    sq = lax.axis_index("seq")
    z, x = dp // NX, dp % NX
    y, c = sq // 2, sq % 2
    e = 2 * x + c
    nseq = 2 * NY
    seqlen = nseq * ROWS
    offset = sq * ROWS

    def dev(d, s):
        return {"dp": d, "seq": s}

    sib = dev(dp, sq + 1 - 2 * c)
    right = dev(dp, (sq + 1) % nseq)
    left = dev(dp, (sq + nseq - 1) % nseq)

    def seq_peer(k):
        return dev(dp, (sq + k) % nseq)

    def y_peer(k):
        return dev(dp, ((y + k) % NY) * 2 + c)

    def z_peer(k):
        return dev(((z + k) % NZ) * NX + x, sq)

    def x_peer(k):
        return dev(z * NX + (x + k) % NX, sq)

    def xc_peer(k):
        other = (e + k) % 8
        return dev(z * NX + other // 2, y * 2 + other % 2)

    barrier = pltpu.get_barrier_semaphore()
    greeted = 0
    for k in range(1, nseq):
        pl.semaphore_signal(barrier, inc=1, device_id=seq_peer(k), device_id_type=MESH)
        greeted += 1
    for k in range(1, NZ):
        pl.semaphore_signal(barrier, inc=1, device_id=z_peer(k), device_id_type=MESH)
        greeted += 1
    for k in range(1, 8):
        pl.semaphore_signal(barrier, inc=1, device_id=xc_peer(k), device_id_type=MESH)
        greeted += 1

    used = [0, 0]
    sends = []

    def remote(src, dst, device):
        index = used[0]
        used[0] += 1
        copy = pltpu.make_async_remote_copy(
            src_ref=src, dst_ref=dst, send_sem=ss.at[index], recv_sem=rs.at[index],
            device_id=device, device_id_type=MESH,
        )
        copy.start()
        sends.append(copy)
        return copy

    def local(src, dst):
        index = used[1]
        used[1] += 1
        copy = pltpu.make_async_copy(src, dst, ls.at[index])
        copy.start()
        return copy

    def cols(g):
        return pl.ds(pl.multiple_of(g * PAIR, PAIR), PAIR)

    wrow = pl.multiple_of(e * HEAD + 16 * z, 16)
    srow = pl.multiple_of((2 * x + 1 - c) * HEAD + 16 * z, 16)
    wown_in = local(wgt.at[pl.ds(wrow, 16), :], wown)
    loads = []
    for g in range(GROUPS):
        loads.append([
            local(feat.at[:, cols(g)], fext.at[g, pl.ds(FHALO, ROWS)]),
            local(key.at[:, cols(g)], kext.at[g, pl.ds(HALF, ROWS)]),
            local(qry.at[:, cols(g)], qv.at[g]),
        ])
    ker_in = local(ker, kerv)
    cot_in = local(cot, cotv)

    pl.semaphore_wait(barrier, greeted)

    w_core = remote(wgt.at[pl.ds(srow, 16), :], wsib, sib)
    halos = []
    for g in range(GROUPS):
        halos.append([
            remote(feat.at[pl.ds(ROWS - FHALO, FHALO), cols(g)], fext.at[g, pl.ds(0, FHALO)], right),
            remote(feat.at[pl.ds(0, FHALO), cols(g)], fext.at[g, pl.ds(FHALO + ROWS, FHALO)], left),
            remote(key.at[pl.ds(ROWS - HALF, HALF), cols(g)], kext.at[g, pl.ds(0, HALF)], right),
            remote(key.at[pl.ds(0, HALF), cols(g)], kext.at[g, pl.ds(HALF + ROWS, HALF)], left),
        ])

    bounds = []
    total = lens[0, 0]
    bounds.append(total)
    for k in range(1, UTT):
        total = total + lens[0, k]
        bounds.append(total)

    def segment(pos):
        seg = jnp.where(pos < 0, -1, 0)
        for bound in bounds:
            seg = seg + jnp.where(pos >= bound, 1, 0)
        return seg

    for r in range(0, FEXT, 64):
        pos = offset - FHALO + r + lax.broadcasted_iota(jnp.int32, (64, HEAD), 0)
        segs[pl.ds(r, 64), :] = segment(pos)
    for r in range(0, EXT, 96):
        center = segs[pl.ds(RIM + r, 96), :]
        for j in range(TAPS):
            near = segs[pl.ds(RIM - REACH + j + r, 96), :]
            taps[j, pl.ds(r, 96), :] = jnp.where(center == near, 1.0, 0.0).astype(F32)
    for b in range(2):
        colpos = offset - HALF + BLKOFF * b + lax.broadcasted_iota(jnp.int32, (8, SPAN), 1)
        seg_col = segment(colpos)[0:1, :]
        seg_row = segs[pl.ds(FHALO + BLK * b, BLK), :]
        seg_row = jnp.concatenate([seg_row] * (SPAN // HEAD), axis=1)
        gap = (
            lax.broadcasted_iota(jnp.int32, (BLK, SPAN), 0) + (BLK * b + HALF - BLKOFF * b)
            - lax.broadcasted_iota(jnp.int32, (BLK, SPAN), 1)
        )
        ok = (seg_row == seg_col) & (gap <= HALF) & (gap >= -HALF)
        bias[b] = jnp.where(ok, 0.0, -jnp.inf).astype(F32)

    wown_in.wait()
    w_core.wait_recv()
    mine = wown[...].astype(F32)
    theirs = wsib[...].astype(F32)
    first = jnp.concatenate([mine, theirs], axis=1)
    second = jnp.concatenate([theirs, mine], axis=1)
    piece = jnp.where(c == 0, first, second).astype(BF16)
    wpiece[...] = piece
    ycol = pl.ds(pl.multiple_of(y * HEAD, HEAD), HEAD)
    wblk[:, ycol] = piece
    w_y = [remote(wpiece, wblk.at[:, ycol], y_peer(k)) for k in range(1, NY)]

    scale = HEAD ** -0.5
    scale2 = scale * math.log2(math.e)

    def forward(g):
        for copy in loads[g]:
            copy.wait()
        for copy in halos[g]:
            copy.wait_recv()
        for j in range(2):
            lanes = pl.ds(j * HEAD, HEAD)
            h = 2 * g + j
            fs[h] = fext[g, :, lanes].astype(F32)
            kw = kerv[:, pl.ds(h * HEAD, HEAD)]
            for r in range(0, EXT, 96):
                acc = kw[REACH:REACH + 1, :] * fs[h, pl.ds(r + RIM, 96), :]
                for t in range(TAPS):
                    if t != REACH:
                        f = fs[h, pl.ds(r + RIM - REACH + t, 96), :]
                        acc = acc + (f * taps[t, pl.ds(r, 96), :]) * kw[t:t + 1, :]
                vext[g, pl.ds(r, 96), lanes] = acc.astype(BF16)
        for j in range(2):
            lanes = pl.ds(j * HEAD, HEAD)
            h = 2 * g + j
            for b in range(2):
                qb = qv[g, pl.ds(BLK * b, BLK), lanes]
                kb = kext[g, pl.ds(BLKOFF * b, SPAN), lanes]
                s = dot(qb, kb, (1, 1)) * scale2 + bias[b]
                top = jnp.max(s, axis=1, keepdims=True)
                ex = jnp.exp2(s - top)
                p = ex * (1.0 / jnp.sum(ex, axis=1, keepdims=True))
                probs[h, b] = p
                vb = vext[g, pl.ds(BLKOFF * b, SPAN), lanes]
                mixed[pl.ds(BLK * b, BLK), pl.ds(h * HEAD, HEAD)] = dot(p.astype(BF16), vb, (1, 0)).astype(BF16)

    ker_in.wait()
    forward(0)

    for copy in w_y:
        copy.wait_recv()
    own_rows = pl.ds(wrow, 16)
    wfull[own_rows, :] = wblk[...]
    w_z = [remote(wblk, wfull.at[own_rows, :], z_peer(k)) for k in range(1, NZ)]

    forward(1)

    for copy in w_z:
        copy.wait_recv()
    head_rows = pl.ds(pl.multiple_of(e * HEAD, HEAD), HEAD)
    w_s = [remote(wfull.at[head_rows, :], wfull.at[head_rows, :], sib)]
    w_x = {}
    for k in (1, 3, 2):
        w_x[k] = remote(wfull.at[head_rows, :], wfull.at[head_rows, :], x_peer(k))

    forward(2)
    forward(3)

    cot_in.wait()
    sib_cols = pl.ds(pl.multiple_of((1 - c) * 512, 512), 512)
    own_cols = pl.ds(pl.multiple_of(c * 512, 512), 512)
    for i in range(NZ):
        mb = mixed[:, pl.ds(i * HEAD, HEAD)]
        gsend[pl.ds(i * HEAD, HEAD), :] = dot(mb, cotv[:, sib_cols], (0, 0)).astype(BF16)
    g_core = remote(gsend, gcore, sib)
    for i in range(NZ):
        mb = mixed[:, pl.ds(i * HEAD, HEAD)]
        gown[pl.ds(i * HEAD, HEAD), :] = dot(mb, cotv[:, own_cols], (0, 0))

    def w_forward(k):
        w_x[k].wait_recv()
        rows = pl.ds(pl.multiple_of((2 * ((x + NX - k) % NX) + c) * HEAD, HEAD), HEAD)
        w_s.append(remote(wfull.at[rows, :], wfull.at[rows, :], sib))

    def backward(step, g):
        w_s[step].wait_recv()
        back = dot(cotv[...], wfull[pl.ds(pl.multiple_of(g * PAIR, PAIR), PAIR), :], (1, 1)).astype(BF16)
        for j in range(2):
            lanes = pl.ds(j * HEAD, HEAD)
            h = 2 * g + j
            bh = back[:, j * HEAD:(j + 1) * HEAD]
            mh = mixed[:, pl.ds(pl.multiple_of(h * HEAD, HEAD), HEAD)]
            inner = jnp.sum(bh.astype(F32) * mh.astype(F32), axis=1, keepdims=True)
            parts = []
            for b in range(2):
                rows = slice(BLK * b, BLK * b + BLK)
                p = probs[h, b]
                kb = kext[g, pl.ds(BLKOFF * b, SPAN), lanes]
                vb = vext[g, pl.ds(BLKOFF * b, SPAN), lanes]
                qb = qv[g, pl.ds(BLK * b, BLK), lanes]
                ds = (p * (dot(bh[rows], vb, (1, 1)) - inner[rows])).astype(BF16)
                dqv[g, pl.ds(BLK * b, BLK), lanes] = (dot(ds, kb, (1, 0)) * scale).astype(BF16)
                parts.append((dot(ds, qb, (0, 0)) * scale, dot(p.astype(BF16), bh[rows], (0, 0))))
            for out, first, second in ((dkx, parts[0][0], parts[1][0]), (dvx, parts[0][1], parts[1][1])):
                out[h, pl.ds(0, BLKOFF), :] = first[:BLKOFF]
                out[h, pl.ds(BLKOFF, SPAN - BLKOFF), :] = first[BLKOFF:] + second[:SPAN - BLKOFF]
                out[h, pl.ds(SPAN, EXT - SPAN), :] = second[SPAN - BLKOFF:]
            dks[step, 0, :, lanes] = dkx[h, pl.ds(0, HALF), :].astype(BF16)
            dks[step, 1, :, lanes] = dkx[h, pl.ds(EXT - HALF, HALF), :].astype(BF16)
            dvs[step, 0, :, lanes] = dvx[h, pl.ds(0, FHALO), :].astype(BF16)
            dvs[step, 1, :, lanes] = dvx[h, pl.ds(EXT - FHALO, FHALO), :].astype(BF16)
        copies = [
            remote(dvs.at[step, 0], dvr.at[step, 0], left),
            remote(dvs.at[step, 1], dvr.at[step, 1], right),
            remote(dks.at[step, 0], dkr.at[step, 0], left),
            remote(dks.at[step, 1], dkr.at[step, 1], right),
        ]
        out = local(dqv.at[g], o_gq.at[:, cols(g)])
        for j in range(2):
            h = 2 * g + j
            sums = [jnp.zeros((8, HEAD), F32) for _ in range(TAPS)]
            for r in range(0, EXT, 96):
                gv = dvx[h, pl.ds(r, 96), :]
                for t in range(TAPS):
                    term = gv * fs[h, pl.ds(r + RIM - REACH + t, 96), :]
                    if t != REACH:
                        term = term * taps[t, pl.ds(r, 96), :]
                    sums[t] = sums[t] + jnp.sum(term.reshape(12, 8, HEAD), axis=0)
            rows = [jnp.sum(v, axis=0, keepdims=True) for v in sums]
            rows.append(jnp.zeros((16 - TAPS, HEAD), F32))
            kp[h] = jnp.concatenate(rows, axis=0)
        return copies, out

    def finish(step, g, copies):
        for copy in copies:
            copy.wait_recv()
        for j in range(2):
            lanes = pl.ds(j * HEAD, HEAD)
            h = 2 * g + j
            dkx[h, pl.ds(HALF, HALF), :] += dkr[step, 1, :, lanes].astype(F32)
            dkx[h, pl.ds(ROWS, HALF), :] += dkr[step, 0, :, lanes].astype(F32)
            dkv[g, :, lanes] = dkx[h, pl.ds(HALF, ROWS), :].astype(BF16)
            dvx[h, pl.ds(HALF - RIM, FHALO), :] += dvr[step, 1, :, lanes].astype(F32)
            dvx[h, pl.ds(ROWS, FHALO), :] += dvr[step, 0, :, lanes].astype(F32)
            kw = kerv[:, pl.ds(pl.multiple_of(h * HEAD, HEAD), HEAD)]
            for r in range(0, ROWS, BLK):
                acc = kw[REACH:REACH + 1, :] * dvx[h, pl.ds(HALF + r, BLK), :]
                for t in range(TAPS):
                    if t != REACH:
                        v = dvx[h, pl.ds(HALF + r - t + REACH, BLK), :]
                        acc = acc + (v * taps[TAPS - 1 - t, pl.ds(HALF + r, BLK), :]) * kw[t:t + 1, :]
                gfv[g, pl.ds(r, BLK), lanes] = acc.astype(BF16)
        return [local(dkv.at[g], o_gk.at[:, cols(g)]), local(gfv.at[g], o_gf.at[:, cols(g)])]

    order = [(0, 0), (1, 1), (2, 3), (3, 2)]
    groups = [(x + NX - k) % NX for _, k in order]
    outs = []
    stages = []

    w_forward(1)
    first, out = backward(0, groups[0])
    outs.append(out)
    stages.append(first)

    g_core.wait_recv()
    for i in range(NZ):
        part = gown[pl.ds(i * HEAD, HEAD), :] + gcore[pl.ds(i * HEAD, HEAD), :].astype(F32)
        gx[i] = part.astype(BF16).reshape(NX, 32, 512)
    g_x = [remote(gx.at[:, (x + k) % NX], gxr.at[k - 1], x_peer(k)) for k in (1, 3, 2)]

    w_forward(3)
    second, out = backward(1, groups[1])
    outs.append(out)
    stages.append(second)
    outs += finish(0, groups[0], stages[0])

    w_forward(2)
    third, out = backward(2, groups[2])
    outs.append(out)
    stages.append(third)
    outs += finish(1, groups[1], stages[1])

    for copy in g_x:
        copy.wait_recv()
    for i in range(NZ):
        part = gx[i, x].astype(F32)
        for k in range(NX - 1):
            part = part + gxr[k, i].astype(F32)
        gz[i] = part.astype(BF16)
    g_z = [remote(gz.at[(z + k) % NZ], gzr.at[k - 1], z_peer(k)) for k in range(1, NZ)]

    fourth, out = backward(3, groups[3])
    outs.append(out)
    stages.append(fourth)

    k_rs = [remote(kp.at[(e + k) % 8], kpr.at[k - 1], xc_peer(k)) for k in range(1, 8)]
    outs += finish(2, groups[2], stages[2])

    for copy in g_z:
        copy.wait_recv()
    part = gz[z].astype(F32)
    for k in range(NZ - 1):
        part = part + gzr[k].astype(F32)
    for s in range(nseq):
        for i in range(4):
            gs[s, pl.ds(2 * i, 2), :] = part[2 * s:2 * s + 2, i * HEAD:(i + 1) * HEAD]
    g_s = [remote(gs.at[(sq + k) % nseq], gsr.at[k - 1], seq_peer(k)) for k in range(1, nseq)]

    for copy in k_rs:
        copy.wait_recv()
    part = kp[e]
    for k in range(7):
        part = part + kpr[k]
    kz[...] = part
    k_z = [remote(kz, kzr.at[k - 1], z_peer(k)) for k in range(1, NZ)]

    outs += finish(3, groups[3], stages[3])

    for copy in k_z:
        copy.wait_recv()
    part = kz[...]
    for k in range(NZ - 1):
        part = part + kzr[k]
    ky[...] = part
    k_y = [remote(ky, kyr.at[k - 1], y_peer(k)) for k in range(1, NY)]

    lay[...] = dot(mixed[...], wfull[...], (1, 0)).astype(BF16)
    outs.append(local(lay, o_layer))

    for copy in k_y:
        copy.wait_recv()
    part = ky[...]
    for k in range(NY - 1):
        part = part + kyr[k]
    part = part * norm
    kall[e] = part
    kfin[...] = part
    k_ag = [remote(kfin, kall.at[e], xc_peer(k)) for k in range(1, 8)]

    for copy in g_s:
        copy.wait_recv()
    same = gs[sq]
    for k in range(2, nseq, 2):
        same = same + gsr[k - 1]
    cross = gsr[0]
    for k in range(3, nseq, 2):
        cross = cross + gsr[k - 1]
    low = jnp.where(c == 0, same, cross) * norm
    high = jnp.where(c == 0, cross, same) * norm
    for i in range(4):
        gwv[:, i * HEAD:(i + 1) * HEAD] = low[2 * i:2 * i + 2, :]
        gwv[:, 512 + i * HEAD:512 + (i + 1) * HEAD] = high[2 * i:2 * i + 2, :]
    outs.append(local(gwv, o_gw))

    for copy in k_ag:
        copy.wait_recv()
    for h in range(8):
        kout[:, h * HEAD:(h + 1) * HEAD] = kall[h, pl.ds(0, TAPS), :]
    outs.append(local(kout, o_gker))
    for copy in outs:
        copy.wait()
    for copy in sends:
        copy.wait_send()


def body(features, queries, key_rows, kernel_taps, out_weight, cotangent, lengths):
    norm = float(lax.axis_size("dp") * lax.axis_size("seq") * ROWS) ** -0.5
    any_spec = pl.BlockSpec(memory_space=pl.ANY)
    sheet = jax.ShapeDtypeStruct((ROWS, WIDTH), BF16)
    v = pltpu.VMEM
    scratch = [
        v((GROUPS, FEXT, PAIR), BF16),
        v((8, FEXT, HEAD), F32),
        v((GROUPS, EXT, PAIR), BF16),
        v((GROUPS, ROWS, PAIR), BF16),
        v((ROWS, WIDTH), BF16),
        v((TAPS, WIDTH), F32),
        v((FEXT, HEAD), jnp.int32),
        v((TAPS, EXT, HEAD), F32),
        v((2, BLK, SPAN), F32),
        v((GROUPS, EXT, PAIR), BF16),
        v((8, 2, BLK, SPAN), F32),
        v((ROWS, WIDTH), BF16),
        v((16, 64), BF16),
        v((16, 64), BF16),
        v((16, HEAD), BF16),
        v((16, WIDTH), BF16),
        v((WIDTH, WIDTH), BF16),
        v((WIDTH, 512), BF16),
        v((WIDTH, 512), F32),
        v((WIDTH, 512), BF16),
        v((NZ, NX, 32, 512), BF16),
        v((NX - 1, NZ, 32, 512), BF16),
        v((NZ, 32, 512), BF16),
        v((NZ - 1, 32, 512), BF16),
        v((16, 8, HEAD), F32),
        v((15, 8, HEAD), F32),
        v((2, WIDTH), F32),
        v((GROUPS, ROWS, PAIR), BF16),
        v((8, EXT, HEAD), F32),
        v((8, EXT, HEAD), F32),
        v((GROUPS, 2, HALF, PAIR), BF16),
        v((GROUPS, 2, FHALO, PAIR), BF16),
        v((GROUPS, 2, HALF, PAIR), BF16),
        v((GROUPS, 2, FHALO, PAIR), BF16),
        v((GROUPS, ROWS, PAIR), BF16),
        v((GROUPS, ROWS, PAIR), BF16),
        v((ROWS, WIDTH), BF16),
        v((8, 16, HEAD), F32),
        v((7, 16, HEAD), F32),
        v((16, HEAD), F32),
        v((NZ - 1, 16, HEAD), F32),
        v((16, HEAD), F32),
        v((NY - 1, 16, HEAD), F32),
        v((16, HEAD), F32),
        v((8, 16, HEAD), F32),
        v((TAPS, WIDTH), F32),
        pltpu.SemaphoreType.DMA((NSEM,)),
        pltpu.SemaphoreType.DMA((NSEM,)),
        pltpu.SemaphoreType.DMA((48,)),
    ]
    layer, grad_q, grad_k, grad_in, grad_kernel, grad_weight = pl.pallas_call(
        functools.partial(kernel, norm),
        out_shape=(
            sheet, sheet, sheet, sheet,
            jax.ShapeDtypeStruct((TAPS, WIDTH), F32),
            jax.ShapeDtypeStruct((2, WIDTH), F32),
        ),
        in_specs=[any_spec] * 6 + [pl.BlockSpec(memory_space=pltpu.SMEM)],
        out_specs=[any_spec] * 6,
        scratch_shapes=scratch,
        compiler_params=pltpu.CompilerParams(
            collective_id=0, has_side_effects=True, vmem_limit_bytes=56 * 1024 * 1024
        ),
        name="block",
    )(features[0], queries[0], key_rows[0], kernel_taps, out_weight, cotangent[0], lengths)
    return (layer[None], grad_q[None], grad_k[None], grad_in[None], grad_kernel, grad_weight)


def solution(mesh):
    sheet = P("dp", "seq", None)
    in_specs = (sheet, sheet, sheet, P(), P(None, "seq"), sheet, P("dp", None))
    out_specs = (sheet, sheet, sheet, sheet, P(), P(("dp", "seq"), None))
    return jax.shard_map(body, mesh=mesh, in_specs=in_specs, out_specs=out_specs, check_vma=False)
```

```python
import functools
import math

import jax
import jax.numpy as jnp
from jax import lax
from jax.experimental import pallas as pl
from jax.experimental.pallas import tpu as pltpu
from jax.sharding import PartitionSpec as P

MESH = pl.DeviceIdType.MESH
F32 = jnp.float32
BF16 = jnp.bfloat16

HALF = 128
TAPS = 9
REACH = 4
RIM = 16
UTT = 16
ROWS = 224
WIDTH = 1024
HEAD = 128
PAIR = 256
GROUPS = 4
NX = 4
NZ = 8
NY = 8
EXT = ROWS + 2 * HALF
FEXT = EXT + 2 * RIM
FHALO = HALF + RIM
BLK = 112
SPAN = 384
BLKOFF = 96
NSEM = 160
KROWS = 48


def dot(a, b, contract):
    return lax.dot_general(a, b, ((contract[:1], contract[1:]), ((), ())), preferred_element_type=F32)


def kernel(
    norm,
    feat, qry, key, ker, wgt, cot, lens,
    o_layer, o_gq, o_gk, o_gf, o_gker, o_gw,
    fext, fs, kext, qv, cotv, kerv, segs, taps, bias, vext, probs, mixed, backv,
    w1, wt,
    gsend, gown, gcore, ga, gar, gb, gbr, gza, gzar, gxb, gxbr, gs, gsr, gfin, gsib, gwv,
    dqv, dkx, dvx, dks, dvs, dkr, dvr, dkv, gfv, lay,
    kp, kpr, kx, kz, ky, kfin, kout,
    ss, rs, ls,
):
    dp = lax.axis_index("dp")
    sq = lax.axis_index("seq")
    z, x = dp // NX, dp % NX
    y, c = sq // 2, sq % 2
    nseq = 2 * NY
    seqlen = nseq * ROWS
    offset = sq * ROWS

    def dev(d, s):
        return {"dp": d, "seq": s}

    sib = dev(dp, sq + 1 - 2 * c)
    right = dev(dp, (sq + 1) % nseq)
    left = dev(dp, (sq + nseq - 1) % nseq)

    def y_peer(k):
        return dev(dp, ((y + k) % NY) * 2 + c)

    def z_peer(k):
        return dev(((z + k) % NZ) * NX + x, sq)

    def x_peer(k):
        return dev(z * NX + (x + k) % NX, sq)

    x_order = (1, 3, 2)
    ring_order = (4, 3, 5, 2, 6, 1, 7)

    barrier = pltpu.get_barrier_semaphore()
    friends = [left, right]
    friends += [y_peer(k) for k in range(1, NY)]
    friends += [z_peer(k) for k in range(1, NZ)]
    friends += [x_peer(k) for k in range(1, NX)]
    for friend in friends:
        pl.semaphore_signal(barrier, inc=1, device_id=friend, device_id_type=MESH)

    used = [0, 0]
    sends = []

    def remote(src, dst, device):
        index = used[0]
        used[0] += 1
        copy = pltpu.make_async_remote_copy(
            src_ref=src, dst_ref=dst, send_sem=ss.at[index], recv_sem=rs.at[index],
            device_id=device, device_id_type=MESH,
        )
        copy.start()
        sends.append(copy)
        return copy

    def local(src, dst):
        index = used[1]
        used[1] += 1
        copy = pltpu.make_async_copy(src, dst, ls.at[index])
        copy.start()
        return copy

    def received(copies):
        for copy in copies:
            copy.wait_recv()

    def cols(g):
        return pl.ds(g * PAIR, PAIR)

    zcol = pl.ds(pl.multiple_of(z * HEAD, HEAD), HEAD)
    w_src = wgt.at[pl.ds(pl.multiple_of(x * 16, 16), 16), zcol]
    w_own = local(w_src, w1.at[y])
    loads = []
    for g in range(GROUPS):
        loads.append([
            local(feat.at[:, cols(g)], fext.at[g, pl.ds(FHALO, ROWS)]),
            local(key.at[:, cols(g)], kext.at[g, pl.ds(HALF, ROWS)]),
            local(qry.at[:, cols(g)], qv.at[g]),
        ])
    ker_in = local(ker, kerv)
    cot_in = local(cot, cotv)

    pl.semaphore_wait(barrier, len(friends))

    w_y = [remote(w_src, w1.at[y], y_peer(k)) for k in ring_order]
    halos = []
    for g in range(GROUPS):
        halos.append([
            remote(feat.at[pl.ds(ROWS - FHALO, FHALO), cols(g)], fext.at[g, pl.ds(0, FHALO)], right),
            remote(feat.at[pl.ds(0, FHALO), cols(g)], fext.at[g, pl.ds(FHALO + ROWS, FHALO)], left),
            remote(key.at[pl.ds(ROWS - HALF, HALF), cols(g)], kext.at[g, pl.ds(0, HALF)], right),
            remote(key.at[pl.ds(0, HALF), cols(g)], kext.at[g, pl.ds(HALF + ROWS, HALF)], left),
        ])

    bounds = []
    total = lens[0, 0]
    bounds.append(total)
    for k in range(1, UTT):
        total = total + lens[0, k]
        bounds.append(total)

    def segment(pos):
        seg = jnp.where(pos < 0, -1, 0)
        for bound in bounds:
            seg = seg + jnp.where(pos >= bound, 1, 0)
        return seg

    for r in range(0, FEXT, 64):
        pos = offset - FHALO + r + lax.broadcasted_iota(jnp.int32, (64, HEAD), 0)
        segs[pl.ds(r, 64), :] = segment(pos)
    for r in range(0, EXT, 96):
        center = segs[pl.ds(RIM + r, 96), :]
        for j in range(TAPS):
            near = segs[pl.ds(RIM - REACH + j + r, 96), :]
            taps[j, pl.ds(r, 96), :] = jnp.where(center == near, 1.0, 0.0).astype(F32)
    for b in range(2):
        colpos = offset - HALF + BLKOFF * b + lax.broadcasted_iota(jnp.int32, (8, SPAN), 1)
        seg_col = segment(colpos)[0:1, :]
        seg_row = segs[pl.ds(FHALO + BLK * b, BLK), :]
        seg_row = jnp.concatenate([seg_row] * (SPAN // HEAD), axis=1)
        gap = (
            lax.broadcasted_iota(jnp.int32, (BLK, SPAN), 0) + (BLK * b + HALF - BLKOFF * b)
            - lax.broadcasted_iota(jnp.int32, (BLK, SPAN), 1)
        )
        ok = (seg_row == seg_col) & (gap <= HALF) & (gap >= -HALF)
        bias[b] = jnp.where(ok, 0.0, -jnp.inf).astype(F32)

    w_own.wait()
    received(w_y)
    near_y, far_y = pl.ds(0, 6), pl.ds(6, 2)
    wt[near_y, c, x, :, zcol] = w1[near_y]
    wt[far_y, c, x, :, zcol] = w1[far_y]
    w_za = [remote(w1.at[near_y], wt.at[near_y, c, x, :, zcol], z_peer(k)) for k in ring_order]
    w_xb = [remote(w1.at[far_y], wt.at[far_y, c, x, :, zcol], x_peer(k)) for k in x_order]

    scale = HEAD ** -0.5
    scale2 = scale * math.log2(math.e)
    sib_cols = pl.ds(pl.multiple_of((1 - c) * 512, 512), 512)
    own_cols = pl.ds(pl.multiple_of(c * 512, 512), 512)

    def forward(g):
        for copy in loads[g]:
            copy.wait()
        received(halos[g])
        for j in range(2):
            lanes = pl.ds(j * HEAD, HEAD)
            h = 2 * g + j
            fs[h] = fext[g, :, lanes].astype(F32)
            kw = kerv[:, pl.ds(h * HEAD, HEAD)]
            for r in range(0, EXT, 96):
                acc = kw[REACH:REACH + 1, :] * fs[h, pl.ds(r + RIM, 96), :]
                for t in range(TAPS):
                    if t != REACH:
                        f = fs[h, pl.ds(r + RIM - REACH + t, 96), :]
                        acc = acc + (f * taps[t, pl.ds(r, 96), :]) * kw[t:t + 1, :]
                vext[g, pl.ds(r, 96), lanes] = acc.astype(BF16)
        for j in range(2):
            lanes = pl.ds(j * HEAD, HEAD)
            h = 2 * g + j
            for b in range(2):
                qb = qv[g, pl.ds(BLK * b, BLK), lanes]
                kb = kext[g, pl.ds(BLKOFF * b, SPAN), lanes]
                s = dot(qb, kb, (1, 1)) * scale2 + bias[b]
                top = jnp.max(s, axis=1, keepdims=True)
                ex = jnp.exp2(s - top)
                p = ex * (1.0 / jnp.sum(ex, axis=1, keepdims=True))
                probs[h, b] = p
                vb = vext[g, pl.ds(BLKOFF * b, SPAN), lanes]
                mixed[pl.ds(BLK * b, BLK), pl.ds(h * HEAD, HEAD)] = dot(p.astype(BF16), vb, (1, 0)).astype(BF16)

    g_core = [None] * GROUPS
    g_xa = []

    def weight_term(g):
        mb = mixed[:, cols(g)]
        gsend[g] = dot(mb, cotv[:, sib_cols], (0, 0)).astype(BF16)
        g_core[g] = remote(gsend.at[g], gcore.at[g], sib)
        gown[g] = dot(mb, cotv[:, own_cols], (0, 0))

    def weight_along_x(g):
        g_core[g].wait_recv()
        for i in range(2):
            half = pl.ds(i * HEAD, HEAD)
            part = (gown[g, half, :] + gcore[g, half, :].astype(F32)).astype(BF16).reshape(NX, 32, 512)
            ga[2 * g + i] = part[:, :, :384]
            gb[2 * g + i] = part[:, :, 384:]
        two = pl.ds(2 * g, 2)
        for k in x_order:
            g_xa.append(remote(ga.at[two, (x + k) % NX], gar.at[k - 1, two], x_peer(k)))

    ker_in.wait()
    forward(0)
    cot_in.wait()
    weight_term(0)

    received(w_za)
    w_s = [remote(wt.at[near_y, c, x], wt.at[near_y, c, x], sib)]
    w_xa = {k: remote(wt.at[near_y, c, x], wt.at[near_y, c, x], x_peer(k)) for k in x_order}
    received(w_xb)
    w_zb = [remote(wt.at[far_y, c, :, :, zcol], wt.at[far_y, c, :, :, zcol], z_peer(k)) for k in ring_order]

    forward(1)
    weight_term(1)
    weight_along_x(0)
    forward(2)
    weight_term(2)
    weight_along_x(1)
    forward(3)
    weight_term(3)
    weight_along_x(2)

    received(w_zb)
    w_s.append(remote(wt.at[far_y, c], wt.at[far_y, c], sib))
    for k in x_order:
        w_xa[k].wait_recv()
        there = (x + NX - k) % NX
        w_s.append(remote(wt.at[near_y, c, there], wt.at[near_y, c, there], sib))

    weight_along_x(3)
    g_zb = [remote(gb.at[(z + k) % NZ], gbr.at[k - 1], z_peer(k)) for k in ring_order]

    received(w_s)
    wide = wt[...].reshape(WIDTH, WIDTH)
    backv[...] = dot(cotv[...], wide, (1, 0)).astype(BF16)

    dv_halos = []
    for g in range(GROUPS):
        for j in range(2):
            lanes = pl.ds(j * HEAD, HEAD)
            h = 2 * g + j
            first, second = [
                dot(probs[h, b].astype(BF16), backv[pl.ds(BLK * b, BLK), pl.ds(h * HEAD, HEAD)], (0, 0)) for b in range(2)
            ]
            dvx[h, pl.ds(0, BLKOFF), :] = first[:BLKOFF]
            dvx[h, pl.ds(BLKOFF, SPAN - BLKOFF), :] = first[BLKOFF:] + second[:SPAN - BLKOFF]
            dvx[h, pl.ds(SPAN, EXT - SPAN), :] = second[SPAN - BLKOFF:]
            sums = [jnp.zeros((8, HEAD), F32) for _ in range(TAPS)]
            for r in range(0, EXT, 96):
                gv = dvx[h, pl.ds(r, 96), :]
                for t in range(TAPS):
                    term = gv * fs[h, pl.ds(r + RIM - REACH + t, 96), :]
                    if t != REACH:
                        term = term * taps[t, pl.ds(r, 96), :]
                    sums[t] = sums[t] + jnp.sum(term.reshape(12, 8, HEAD), axis=0)
            rows = jnp.concatenate([jnp.sum(v, axis=0, keepdims=True) for v in sums], axis=0)
            kp[h // 4, pl.ds((h % 4) * TAPS, TAPS), :] = rows
            dvs[g, 0, :, lanes] = dvx[h, pl.ds(0, FHALO), :].astype(BF16)
            dvs[g, 1, :, lanes] = dvx[h, pl.ds(EXT - FHALO, FHALO), :].astype(BF16)
    k_sib = remote(kp.at[1 - c], kpr, sib)
    for g in range(GROUPS):
        dv_halos.append([
            remote(dvs.at[g, 0], dvr.at[g, 0], left),
            remote(dvs.at[g, 1], dvr.at[g, 1], right),
        ])

    outs = []
    dk_halos = []

    def backward(g):
        for j in range(2):
            lanes = pl.ds(j * HEAD, HEAD)
            h = 2 * g + j
            bh = backv[:, pl.ds(h * HEAD, HEAD)]
            mh = mixed[:, pl.ds(h * HEAD, HEAD)]
            inner = jnp.sum(bh.astype(F32) * mh.astype(F32), axis=1, keepdims=True)
            parts = []
            for b in range(2):
                rows = slice(BLK * b, BLK * b + BLK)
                kb = kext[g, pl.ds(BLKOFF * b, SPAN), lanes]
                vb = vext[g, pl.ds(BLKOFF * b, SPAN), lanes]
                qb = qv[g, pl.ds(BLK * b, BLK), lanes]
                ds = (probs[h, b] * (dot(bh[rows], vb, (1, 1)) - inner[rows])).astype(BF16)
                dqv[g, pl.ds(BLK * b, BLK), lanes] = (dot(ds, kb, (1, 0)) * scale).astype(BF16)
                parts.append(dot(ds, qb, (0, 0)) * scale)
            first, second = parts
            dkx[h, pl.ds(0, BLKOFF), :] = first[:BLKOFF]
            dkx[h, pl.ds(BLKOFF, SPAN - BLKOFF), :] = first[BLKOFF:] + second[:SPAN - BLKOFF]
            dkx[h, pl.ds(SPAN, EXT - SPAN), :] = second[SPAN - BLKOFF:]
            dks[g, 0, :, lanes] = dkx[h, pl.ds(0, HALF), :].astype(BF16)
            dks[g, 1, :, lanes] = dkx[h, pl.ds(EXT - HALF, HALF), :].astype(BF16)
        dk_halos.append([
            remote(dks.at[g, 0], dkr.at[g, 0], left),
            remote(dks.at[g, 1], dkr.at[g, 1], right),
        ])
        outs.append(local(dqv.at[g], o_gq.at[:, cols(g)]))

    def finish(g):
        received(dv_halos[g])
        for j in range(2):
            lanes = pl.ds(j * HEAD, HEAD)
            h = 2 * g + j
            dvx[h, pl.ds(HALF - RIM, FHALO), :] += dvr[g, 1, :, lanes].astype(F32)
            dvx[h, pl.ds(ROWS, FHALO), :] += dvr[g, 0, :, lanes].astype(F32)
            kw = kerv[:, pl.ds(h * HEAD, HEAD)]
            for r in range(0, ROWS, BLK):
                acc = kw[REACH:REACH + 1, :] * dvx[h, pl.ds(HALF + r, BLK), :]
                for t in range(TAPS):
                    if t != REACH:
                        v = dvx[h, pl.ds(HALF + r - t + REACH, BLK), :]
                        acc = acc + (v * taps[TAPS - 1 - t, pl.ds(HALF + r, BLK), :]) * kw[t:t + 1, :]
                gfv[g, pl.ds(r, BLK), lanes] = acc.astype(BF16)
        outs.append(local(gfv.at[g], o_gf.at[:, cols(g)]))
        received(dk_halos[g])
        for j in range(2):
            lanes = pl.ds(j * HEAD, HEAD)
            h = 2 * g + j
            dkx[h, pl.ds(HALF, HALF), :] += dkr[g, 1, :, lanes].astype(F32)
            dkx[h, pl.ds(ROWS, HALF), :] += dkr[g, 0, :, lanes].astype(F32)
            dkv[g, :, lanes] = dkx[h, pl.ds(HALF, ROWS), :].astype(BF16)
        outs.append(local(dkv.at[g], o_gk.at[:, cols(g)]))

    backward(0)
    k_sib.wait_recv()
    kx[x] = kp[c] + kpr[...]
    k_x = [remote(kx.at[x], kx.at[x], x_peer(k)) for k in x_order]

    received(g_xa)
    for i in range(NZ):
        part = ga[i, x].astype(F32)
        for k in range(NX - 1):
            part = part + gar[k, i].astype(F32)
        gza[i] = part.astype(BF16)
    g_za = [remote(gza.at[(z + k) % NZ], gzar.at[k - 1], z_peer(k)) for k in ring_order]
    received(g_zb)
    for i in range(NX):
        part = gb[z, i].astype(F32)
        for k in range(NZ - 1):
            part = part + gbr[k, i].astype(F32)
        gxb[i] = part.astype(BF16)
    g_xb = [remote(gxb.at[(x + k) % NX], gxbr.at[k - 1], x_peer(k)) for k in x_order]

    backward(1)
    received(k_x)
    kz[z] = (kx[0] + kx[1] + kx[2] + kx[3]).astype(BF16)
    k_z = [remote(kz.at[z], kz.at[z], z_peer(k)) for k in ring_order]

    backward(2)
    backward(3)
    finish(0)

    received(k_z)
    part = kz[0].astype(F32)
    for k in range(1, NZ):
        part = part + kz[k].astype(F32)
    ky[y] = part.astype(BF16)
    k_y = [remote(ky.at[y], ky.at[y], y_peer(k)) for k in ring_order]

    finish(1)

    received(g_za)
    received(g_xb)
    part = gza[z].astype(F32)
    for k in range(NZ - 1):
        part = part + gzar[k].astype(F32)
    last = gxb[x].astype(F32)
    for k in range(NX - 1):
        last = last + gxbr[k].astype(F32)
    part = jnp.concatenate([part, last], axis=1)
    for s in range(NY):
        for i in range(4):
            gs[s, pl.ds(4 * i, 4), :] = part[4 * s:4 * s + 4, i * HEAD:(i + 1) * HEAD]
    g_y = [remote(gs.at[(y + k) % NY], gsr.at[k - 1], y_peer(k)) for k in ring_order]

    finish(2)
    finish(3)
    lay[...] = dot(mixed[...], wt[...].reshape(WIDTH, WIDTH), (1, 1)).astype(BF16)
    outs.append(local(lay, o_layer))

    received(k_y)
    part = ky[0].astype(F32)
    for k in range(1, NY):
        part = part + ky[k].astype(F32)
    kfin[c] = part * norm
    k_last = remote(kfin.at[c], kfin.at[c], sib)

    received(g_y)
    part = gs[y]
    for k in range(NY - 1):
        part = part + gsr[k]
    gfin[...] = part * norm
    g_last = remote(gfin, gsib, sib)

    k_last.wait_recv()
    for h in range(8):
        kout[:, h * HEAD:(h + 1) * HEAD] = kfin[h // 4, pl.ds((h % 4) * TAPS, TAPS), :]
    outs.append(local(kout, o_gker))

    g_last.wait_recv()
    mine, theirs = gfin[...], gsib[...]
    low = jnp.where(c == 0, mine, theirs)
    high = jnp.where(c == 0, theirs, mine)
    for n, half in enumerate((low, high)):
        for i in range(4):
            rows = jnp.where(c == 0, half[4 * i:4 * i + 2, :], half[4 * i + 2:4 * i + 4, :])
            gwv[:, n * 512 + i * HEAD:n * 512 + (i + 1) * HEAD] = rows
    outs.append(local(gwv, o_gw))

    for copy in outs:
        copy.wait()
    for copy in sends:
        copy.wait_send()


def hand_over(*refs):
    given, out, held, sem = refs[:6], refs[6:12], refs[12:18], refs[18]
    loads = [pltpu.make_async_copy(given[i], held[i], sem.at[i]) for i in range(6)]
    stores = [pltpu.make_async_copy(held[i], out[i], sem.at[6 + i]) for i in range(6)]
    for copy in loads:
        copy.start()
    for load, store in zip(loads, stores):
        load.wait()
        store.start()
    for copy in stores:
        copy.wait()


def body(features, queries, key_rows, kernel_taps, out_weight, cotangent, lengths):
    norm = float(lax.axis_size("dp") * lax.axis_size("seq") * ROWS) ** -0.5
    any_spec = pl.BlockSpec(memory_space=pl.ANY)
    sheet = jax.ShapeDtypeStruct((ROWS, WIDTH), BF16)
    v = pltpu.VMEM
    scratch = [
        v((GROUPS, FEXT, PAIR), BF16),
        v((8, FEXT, HEAD), F32),
        v((GROUPS, EXT, PAIR), BF16),
        v((GROUPS, ROWS, PAIR), BF16),
        v((ROWS, WIDTH), BF16),
        v((TAPS, WIDTH), F32),
        v((FEXT, HEAD), jnp.int32),
        v((TAPS, EXT, HEAD), F32),
        v((2, BLK, SPAN), F32),
        v((GROUPS, EXT, PAIR), BF16),
        v((8, 2, BLK, SPAN), F32),
        v((ROWS, WIDTH), BF16),
        v((ROWS, WIDTH), BF16),
        v((NY, 16, HEAD), BF16),
        v((NY, 2, NX, 16, WIDTH), BF16),
        v((GROUPS, PAIR, 512), BF16),
        v((GROUPS, PAIR, 512), F32),
        v((GROUPS, PAIR, 512), BF16),
        v((NZ, NX, 32, 384), BF16),
        v((NX - 1, NZ, 32, 384), BF16),
        v((NZ, NX, 32, 128), BF16),
        v((NZ - 1, NX, 32, 128), BF16),
        v((NZ, 32, 384), BF16),
        v((NZ - 1, 32, 384), BF16),
        v((NX, 32, 128), BF16),
        v((NX - 1, 32, 128), BF16),
        v((NY, 16, HEAD), F32),
        v((NY - 1, 16, HEAD), F32),
        v((16, HEAD), F32),
        v((16, HEAD), F32),
        v((2, WIDTH), F32),
        v((GROUPS, ROWS, PAIR), BF16),
        v((8, EXT, HEAD), F32),
        v((8, EXT, HEAD), F32),
        v((GROUPS, 2, HALF, PAIR), BF16),
        v((GROUPS, 2, FHALO, PAIR), BF16),
        v((GROUPS, 2, HALF, PAIR), BF16),
        v((GROUPS, 2, FHALO, PAIR), BF16),
        v((GROUPS, ROWS, PAIR), BF16),
        v((GROUPS, ROWS, PAIR), BF16),
        v((ROWS, WIDTH), BF16),
        v((2, KROWS, HEAD), F32),
        v((KROWS, HEAD), F32),
        v((NX, KROWS, HEAD), F32),
        v((NZ, KROWS, HEAD), BF16),
        v((NY, KROWS, HEAD), BF16),
        v((2, KROWS, HEAD), F32),
        v((TAPS, WIDTH), F32),
        pltpu.SemaphoreType.DMA((NSEM,)),
        pltpu.SemaphoreType.DMA((NSEM,)),
        pltpu.SemaphoreType.DMA((48,)),
    ]
    shapes = (
        sheet, sheet, sheet, sheet,
        jax.ShapeDtypeStruct((TAPS, WIDTH), F32),
        jax.ShapeDtypeStruct((2, WIDTH), F32),
    )
    results = pl.pallas_call(
        functools.partial(kernel, norm),
        out_shape=shapes,
        in_specs=[any_spec] * 6 + [pl.BlockSpec(memory_space=pltpu.SMEM)],
        out_specs=[any_spec] * 6,
        scratch_shapes=scratch,
        compiler_params=pltpu.CompilerParams(
            collective_id=0, has_side_effects=True, vmem_limit_bytes=56 * 1024 * 1024
        ),
        name="block",
    )(features[0], queries[0], key_rows[0], kernel_taps, out_weight.T, cotangent[0], lengths)
    layer, grad_q, grad_k, grad_in, grad_kernel, grad_weight = pl.pallas_call(
        hand_over,
        out_shape=shapes,
        in_specs=[any_spec] * 6,
        out_specs=[any_spec] * 6,
        scratch_shapes=[v(shape.shape, shape.dtype) for shape in shapes] + [pltpu.SemaphoreType.DMA((12,))],
        name="hand_over",
    )(*results)
    return (layer[None], grad_q[None], grad_k[None], grad_in[None], grad_kernel, grad_weight)


def solution(mesh):
    sheet = P("dp", "seq", None)
    in_specs = (sheet, sheet, sheet, P(), P(None, "seq"), sheet, P("dp", None))
    out_specs = (sheet, sheet, sheet, sheet, P(), P(("dp", "seq"), None))
    return jax.shard_map(body, mesh=mesh, in_specs=in_specs, out_specs=out_specs, check_vma=False)
```

```python
import functools
import math

import jax
import jax.numpy as jnp
from jax import lax
from jax.experimental import pallas as pl
from jax.experimental.pallas import tpu as pltpu
from jax.sharding import PartitionSpec as P

MESH = pl.DeviceIdType.MESH
F32 = jnp.float32
BF16 = jnp.bfloat16

HALF = 128
TAPS = 9
REACH = 4
RIM = 16
UTT = 16
ROWS = 224
WIDTH = 1024
HEAD = 128
PAIR = 256
GROUPS = 4
NX = 4
NZ = 8
NY = 8
EXT = ROWS + 2 * HALF
FEXT = EXT + 2 * RIM
FHALO = HALF + RIM
BLK = 112
SPAN = 384
BLKOFF = 96
NSEM = 160
KROWS = 48


def dot(a, b, contract):
    return lax.dot_general(a, b, ((contract[:1], contract[1:]), ((), ())), preferred_element_type=F32)


def kernel(
    norm,
    feat, qry, key, ker, wgt, cot, lens,
    o_layer, o_gq, o_gk, o_gf, o_gker, o_gw,
    fext, fs, kext, qv, cotv, kerv, segs, taps, bias, vext, probs, mixed, backv,
    w1, wt,
    gsend, gown, gcore, ga, gar, gb, gbr, gza, gzar, gxb, gxbr, gs, gsr, gfin, gsib, gwv,
    dqv, dkx, dvx, dks, dvs, dkr, dvr, dkv, gfv, lay,
    kp, kpr, kx, kz, ky, kfin, kout,
    ss, rs, ls,
):
    dp = lax.axis_index("dp")
    sq = lax.axis_index("seq")
    z, x = dp // NX, dp % NX
    y, c = sq // 2, sq % 2
    nseq = 2 * NY
    seqlen = nseq * ROWS
    offset = sq * ROWS

    def dev(d, s):
        return {"dp": d, "seq": s}

    sib = dev(dp, sq + 1 - 2 * c)
    right = dev(dp, (sq + 1) % nseq)
    left = dev(dp, (sq + nseq - 1) % nseq)

    def y_peer(k):
        return dev(dp, ((y + k) % NY) * 2 + c)

    def z_peer(k):
        return dev(((z + k) % NZ) * NX + x, sq)

    def x_peer(k):
        return dev(z * NX + (x + k) % NX, sq)

    x_order = (1, 3, 2)
    ring_order = (4, 3, 5, 2, 6, 1, 7)

    barrier = pltpu.get_barrier_semaphore()
    friends = [left, right]
    friends += [y_peer(k) for k in range(1, NY)]
    friends += [z_peer(k) for k in range(1, NZ)]
    friends += [x_peer(k) for k in range(1, NX)]
    for friend in friends:
        pl.semaphore_signal(barrier, inc=1, device_id=friend, device_id_type=MESH)

    used = [0, 0]
    sends = []

    def remote(src, dst, device):
        index = used[0]
        used[0] += 1
        copy = pltpu.make_async_remote_copy(
            src_ref=src, dst_ref=dst, send_sem=ss.at[index], recv_sem=rs.at[index],
            device_id=device, device_id_type=MESH,
        )
        copy.start()
        sends.append(copy)
        return copy

    def local(src, dst):
        index = used[1]
        used[1] += 1
        copy = pltpu.make_async_copy(src, dst, ls.at[index])
        copy.start()
        return copy

    def received(copies):
        for copy in copies:
            copy.wait_recv()

    def cols(g):
        return pl.ds(g * PAIR, PAIR)

    zcol = pl.ds(pl.multiple_of(z * HEAD, HEAD), HEAD)
    w_src = wgt.at[pl.ds(pl.multiple_of(x * 16, 16), 16), zcol]
    w_own = local(w_src, w1.at[y])
    far = (x + 2) % NX
    far_src = wgt.at[pl.ds(pl.multiple_of(far * 16, 16), 16), :]
    far_own = local(far_src, wt.at[y, c, far])
    loads = []
    for g in range(GROUPS):
        loads.append([
            local(feat.at[:, cols(g)], fext.at[g, pl.ds(FHALO, ROWS)]),
            local(key.at[:, cols(g)], kext.at[g, pl.ds(HALF, ROWS)]),
            local(qry.at[:, cols(g)], qv.at[g]),
        ])
    ker_in = local(ker, kerv)
    cot_in = local(cot, cotv)

    pl.semaphore_wait(barrier, len(friends))

    w_y = [remote(w_src, w1.at[y], y_peer(k)) for k in ring_order]
    halos = []
    for g in range(GROUPS):
        halos.append([
            remote(feat.at[pl.ds(ROWS - FHALO, FHALO), cols(g)], fext.at[g, pl.ds(0, FHALO)], right),
            remote(feat.at[pl.ds(0, FHALO), cols(g)], fext.at[g, pl.ds(FHALO + ROWS, FHALO)], left),
            remote(key.at[pl.ds(ROWS - HALF, HALF), cols(g)], kext.at[g, pl.ds(0, HALF)], right),
            remote(key.at[pl.ds(0, HALF), cols(g)], kext.at[g, pl.ds(HALF + ROWS, HALF)], left),
        ])

    w_far = [remote(far_src, wt.at[y, c, far], y_peer(k)) for k in ring_order]

    bounds = []
    total = lens[0, 0]
    bounds.append(total)
    for k in range(1, UTT):
        total = total + lens[0, k]
        bounds.append(total)

    def segment(pos):
        seg = jnp.where(pos < 0, -1, 0)
        for bound in bounds:
            seg = seg + jnp.where(pos >= bound, 1, 0)
        return seg

    for r in range(0, FEXT, 64):
        pos = offset - FHALO + r + lax.broadcasted_iota(jnp.int32, (64, HEAD), 0)
        segs[pl.ds(r, 64), :] = segment(pos)
    for r in range(0, EXT, 96):
        center = segs[pl.ds(RIM + r, 96), :]
        for j in range(TAPS):
            near = segs[pl.ds(RIM - REACH + j + r, 96), :]
            taps[j, pl.ds(r, 96), :] = jnp.where(center == near, 1.0, 0.0).astype(F32)
    for b in range(2):
        colpos = offset - HALF + BLKOFF * b + lax.broadcasted_iota(jnp.int32, (8, SPAN), 1)
        seg_col = segment(colpos)[0:1, :]
        seg_row = segs[pl.ds(FHALO + BLK * b, BLK), :]
        seg_row = jnp.concatenate([seg_row] * (SPAN // HEAD), axis=1)
        gap = (
            lax.broadcasted_iota(jnp.int32, (BLK, SPAN), 0) + (BLK * b + HALF - BLKOFF * b)
            - lax.broadcasted_iota(jnp.int32, (BLK, SPAN), 1)
        )
        ok = (seg_row == seg_col) & (gap <= HALF) & (gap >= -HALF)
        bias[b] = jnp.where(ok, 0.0, -jnp.inf).astype(F32)

    w_own.wait()
    received(w_y)
    wt[:, c, x, :, zcol] = w1[...]
    w_z = [remote(w1, wt.at[:, c, x, :, zcol], z_peer(k)) for k in ring_order]

    scale = HEAD ** -0.5
    scale2 = scale * math.log2(math.e)
    sib_cols = pl.ds(pl.multiple_of((1 - c) * 512, 512), 512)
    own_cols = pl.ds(pl.multiple_of(c * 512, 512), 512)

    def forward(g):
        for copy in loads[g]:
            copy.wait()
        received(halos[g])
        for j in range(2):
            lanes = pl.ds(j * HEAD, HEAD)
            h = 2 * g + j
            fs[h] = fext[g, :, lanes].astype(F32)
            kw = kerv[:, pl.ds(h * HEAD, HEAD)]
            for r in range(0, EXT, 96):
                acc = kw[REACH:REACH + 1, :] * fs[h, pl.ds(r + RIM, 96), :]
                for t in range(TAPS):
                    if t != REACH:
                        f = fs[h, pl.ds(r + RIM - REACH + t, 96), :]
                        acc = acc + (f * taps[t, pl.ds(r, 96), :]) * kw[t:t + 1, :]
                vext[g, pl.ds(r, 96), lanes] = acc.astype(BF16)
        for j in range(2):
            lanes = pl.ds(j * HEAD, HEAD)
            h = 2 * g + j
            for b in range(2):
                qb = qv[g, pl.ds(BLK * b, BLK), lanes]
                kb = kext[g, pl.ds(BLKOFF * b, SPAN), lanes]
                s = dot(qb, kb, (1, 1)) * scale2 + bias[b]
                top = jnp.max(s, axis=1, keepdims=True)
                ex = jnp.exp2(s - top)
                p = ex * (1.0 / jnp.sum(ex, axis=1, keepdims=True))
                probs[h, b] = p
                vb = vext[g, pl.ds(BLKOFF * b, SPAN), lanes]
                mixed[pl.ds(BLK * b, BLK), pl.ds(h * HEAD, HEAD)] = dot(p.astype(BF16), vb, (1, 0)).astype(BF16)

    g_core = [None] * GROUPS
    g_xa = []

    def weight_term(g):
        mb = mixed[:, cols(g)]
        gsend[g] = dot(mb, cotv[:, sib_cols], (0, 0)).astype(BF16)
        g_core[g] = remote(gsend.at[g], gcore.at[g], sib)
        gown[g] = dot(mb, cotv[:, own_cols], (0, 0))

    def weight_along_x(g):
        g_core[g].wait_recv()
        for i in range(2):
            half = pl.ds(i * HEAD, HEAD)
            part = (gown[g, half, :] + gcore[g, half, :].astype(F32)).astype(BF16).reshape(NX, 32, 512)
            ga[2 * g + i] = part[:, :, :384]
            gb[2 * g + i] = part[:, :, 384:]
        two = pl.ds(2 * g, 2)
        for k in x_order:
            g_xa.append(remote(ga.at[two, (x + k) % NX], gar.at[k - 1, two], x_peer(k)))

    ker_in.wait()
    forward(0)
    cot_in.wait()
    weight_term(0)

    w_s = []

    def to_sibling(there):
        w_s.append(remote(wt.at[:, c, there], wt.at[:, c, there], sib))

    received(w_z)
    w_x = {k: remote(wt.at[:, c, x], wt.at[:, c, x], x_peer(k)) for k in (1, 3)}
    to_sibling(x)

    forward(1)
    weight_term(1)
    weight_along_x(0)
    forward(2)
    weight_term(2)
    weight_along_x(1)
    forward(3)
    weight_term(3)
    weight_along_x(2)

    weight_along_x(3)
    g_zb = [remote(gb.at[(z + k) % NZ], gbr.at[k - 1], z_peer(k)) for k in ring_order]

    far_own.wait()
    received(w_far)
    to_sibling(far)
    for k in (1, 3):
        w_x[k].wait_recv()
        to_sibling((x + NX - k) % NX)

    received(w_s)
    wide = wt[...].reshape(WIDTH, WIDTH)
    backv[...] = dot(cotv[...], wide, (1, 0)).astype(BF16)

    dv_halos = []
    for g in range(GROUPS):
        for j in range(2):
            lanes = pl.ds(j * HEAD, HEAD)
            h = 2 * g + j
            first, second = [
                dot(probs[h, b].astype(BF16), backv[pl.ds(BLK * b, BLK), pl.ds(h * HEAD, HEAD)], (0, 0)) for b in range(2)
            ]
            dvx[h, pl.ds(0, BLKOFF), :] = first[:BLKOFF]
            dvx[h, pl.ds(BLKOFF, SPAN - BLKOFF), :] = first[BLKOFF:] + second[:SPAN - BLKOFF]
            dvx[h, pl.ds(SPAN, EXT - SPAN), :] = second[SPAN - BLKOFF:]
            sums = [jnp.zeros((8, HEAD), F32) for _ in range(TAPS)]
            for r in range(0, EXT, 96):
                gv = dvx[h, pl.ds(r, 96), :]
                for t in range(TAPS):
                    term = gv * fs[h, pl.ds(r + RIM - REACH + t, 96), :]
                    if t != REACH:
                        term = term * taps[t, pl.ds(r, 96), :]
                    sums[t] = sums[t] + jnp.sum(term.reshape(12, 8, HEAD), axis=0)
            rows = jnp.concatenate([jnp.sum(v, axis=0, keepdims=True) for v in sums], axis=0)
            kp[h // 4, pl.ds((h % 4) * TAPS, TAPS), :] = rows
            dvs[g, 0, :, lanes] = dvx[h, pl.ds(0, FHALO), :].astype(BF16)
            dvs[g, 1, :, lanes] = dvx[h, pl.ds(EXT - FHALO, FHALO), :].astype(BF16)
    k_sib = remote(kp.at[1 - c], kpr, sib)
    for g in range(GROUPS):
        dv_halos.append([
            remote(dvs.at[g, 0], dvr.at[g, 0], left),
            remote(dvs.at[g, 1], dvr.at[g, 1], right),
        ])

    outs = []
    dk_halos = []

    def backward(g):
        for j in range(2):
            lanes = pl.ds(j * HEAD, HEAD)
            h = 2 * g + j
            bh = backv[:, pl.ds(h * HEAD, HEAD)]
            mh = mixed[:, pl.ds(h * HEAD, HEAD)]
            inner = jnp.sum(bh.astype(F32) * mh.astype(F32), axis=1, keepdims=True)
            parts = []
            for b in range(2):
                rows = slice(BLK * b, BLK * b + BLK)
                kb = kext[g, pl.ds(BLKOFF * b, SPAN), lanes]
                vb = vext[g, pl.ds(BLKOFF * b, SPAN), lanes]
                qb = qv[g, pl.ds(BLK * b, BLK), lanes]
                ds = (probs[h, b] * (dot(bh[rows], vb, (1, 1)) - inner[rows])).astype(BF16)
                dqv[g, pl.ds(BLK * b, BLK), lanes] = (dot(ds, kb, (1, 0)) * scale).astype(BF16)
                parts.append(dot(ds, qb, (0, 0)) * scale)
            first, second = parts
            dkx[h, pl.ds(0, BLKOFF), :] = first[:BLKOFF]
            dkx[h, pl.ds(BLKOFF, SPAN - BLKOFF), :] = first[BLKOFF:] + second[:SPAN - BLKOFF]
            dkx[h, pl.ds(SPAN, EXT - SPAN), :] = second[SPAN - BLKOFF:]
            dks[g, 0, :, lanes] = dkx[h, pl.ds(0, HALF), :].astype(BF16)
            dks[g, 1, :, lanes] = dkx[h, pl.ds(EXT - HALF, HALF), :].astype(BF16)
        dk_halos.append([
            remote(dks.at[g, 0], dkr.at[g, 0], left),
            remote(dks.at[g, 1], dkr.at[g, 1], right),
        ])
        outs.append(local(dqv.at[g], o_gq.at[:, cols(g)]))

    def finish(g):
        received(dv_halos[g])
        for j in range(2):
            lanes = pl.ds(j * HEAD, HEAD)
            h = 2 * g + j
            dvx[h, pl.ds(HALF - RIM, FHALO), :] += dvr[g, 1, :, lanes].astype(F32)
            dvx[h, pl.ds(ROWS, FHALO), :] += dvr[g, 0, :, lanes].astype(F32)
            kw = kerv[:, pl.ds(h * HEAD, HEAD)]
            for r in range(0, ROWS, BLK):
                acc = kw[REACH:REACH + 1, :] * dvx[h, pl.ds(HALF + r, BLK), :]
                for t in range(TAPS):
                    if t != REACH:
                        v = dvx[h, pl.ds(HALF + r - t + REACH, BLK), :]
                        acc = acc + (v * taps[TAPS - 1 - t, pl.ds(HALF + r, BLK), :]) * kw[t:t + 1, :]
                gfv[g, pl.ds(r, BLK), lanes] = acc.astype(BF16)
        outs.append(local(gfv.at[g], o_gf.at[:, cols(g)]))
        received(dk_halos[g])
        for j in range(2):
            lanes = pl.ds(j * HEAD, HEAD)
            h = 2 * g + j
            dkx[h, pl.ds(HALF, HALF), :] += dkr[g, 1, :, lanes].astype(F32)
            dkx[h, pl.ds(ROWS, HALF), :] += dkr[g, 0, :, lanes].astype(F32)
            dkv[g, :, lanes] = dkx[h, pl.ds(HALF, ROWS), :].astype(BF16)
        outs.append(local(dkv.at[g], o_gk.at[:, cols(g)]))

    backward(0)
    k_sib.wait_recv()
    kx[x] = kp[c] + kpr[...]
    k_x = [remote(kx.at[x], kx.at[x], x_peer(k)) for k in x_order]

    received(g_xa)
    for i in range(NZ):
        part = ga[i, x].astype(F32)
        for k in range(NX - 1):
            part = part + gar[k, i].astype(F32)
        gza[i] = part.astype(BF16)
    g_za = [remote(gza.at[(z + k) % NZ], gzar.at[k - 1], z_peer(k)) for k in ring_order]
    received(g_zb)
    for i in range(NX):
        part = gb[z, i].astype(F32)
        for k in range(NZ - 1):
            part = part + gbr[k, i].astype(F32)
        gxb[i] = part.astype(BF16)
    g_xb = [remote(gxb.at[(x + k) % NX], gxbr.at[k - 1], x_peer(k)) for k in x_order]

    backward(1)
    received(k_x)
    kz[z] = (kx[0] + kx[1] + kx[2] + kx[3]).astype(BF16)
    k_z = [remote(kz.at[z], kz.at[z], z_peer(k)) for k in ring_order]

    backward(2)
    backward(3)
    finish(0)

    received(k_z)
    part = kz[0].astype(F32)
    for k in range(1, NZ):
        part = part + kz[k].astype(F32)
    ky[y] = part.astype(BF16)
    k_y = [remote(ky.at[y], ky.at[y], y_peer(k)) for k in ring_order]

    finish(1)

    received(g_za)
    received(g_xb)
    part = gza[z].astype(F32)
    for k in range(NZ - 1):
        part = part + gzar[k].astype(F32)
    last = gxb[x].astype(F32)
    for k in range(NX - 1):
        last = last + gxbr[k].astype(F32)
    part = jnp.concatenate([part, last], axis=1)
    for s in range(NY):
        for i in range(4):
            gs[s, pl.ds(4 * i, 4), :] = part[4 * s:4 * s + 4, i * HEAD:(i + 1) * HEAD]
    g_y = [remote(gs.at[(y + k) % NY], gsr.at[k - 1], y_peer(k)) for k in ring_order]

    finish(2)
    finish(3)
    lay[...] = dot(mixed[...], wt[...].reshape(WIDTH, WIDTH), (1, 1)).astype(BF16)
    outs.append(local(lay, o_layer))

    received(k_y)
    part = ky[0].astype(F32)
    for k in range(1, NY):
        part = part + ky[k].astype(F32)
    kfin[c] = part * norm
    k_last = remote(kfin.at[c], kfin.at[c], sib)

    received(g_y)
    part = gs[y]
    for k in range(NY - 1):
        part = part + gsr[k]
    gfin[...] = part * norm
    g_last = remote(gfin, gsib, sib)

    k_last.wait_recv()
    for h in range(8):
        kout[:, h * HEAD:(h + 1) * HEAD] = kfin[h // 4, pl.ds((h % 4) * TAPS, TAPS), :]
    outs.append(local(kout, o_gker))

    g_last.wait_recv()
    mine, theirs = gfin[...], gsib[...]
    low = jnp.where(c == 0, mine, theirs)
    high = jnp.where(c == 0, theirs, mine)
    for n, half in enumerate((low, high)):
        for i in range(4):
            rows = jnp.where(c == 0, half[4 * i:4 * i + 2, :], half[4 * i + 2:4 * i + 4, :])
            gwv[:, n * 512 + i * HEAD:n * 512 + (i + 1) * HEAD] = rows
    outs.append(local(gwv, o_gw))

    for copy in outs:
        copy.wait()
    for copy in sends:
        copy.wait_send()


def hand_over(*refs):
    given, out, held, sem = refs[:6], refs[6:12], refs[12:18], refs[18]
    loads = [pltpu.make_async_copy(given[i], held[i], sem.at[i]) for i in range(6)]
    stores = [pltpu.make_async_copy(held[i], out[i], sem.at[6 + i]) for i in range(6)]
    for copy in loads:
        copy.start()
    for load, store in zip(loads, stores):
        load.wait()
        store.start()
    for copy in stores:
        copy.wait()


def body(features, queries, key_rows, kernel_taps, out_weight, cotangent, lengths):
    norm = float(lax.axis_size("dp") * lax.axis_size("seq") * ROWS) ** -0.5
    any_spec = pl.BlockSpec(memory_space=pl.ANY)
    sheet = jax.ShapeDtypeStruct((ROWS, WIDTH), BF16)
    v = pltpu.VMEM
    scratch = [
        v((GROUPS, FEXT, PAIR), BF16),
        v((8, FEXT, HEAD), F32),
        v((GROUPS, EXT, PAIR), BF16),
        v((GROUPS, ROWS, PAIR), BF16),
        v((ROWS, WIDTH), BF16),
        v((TAPS, WIDTH), F32),
        v((FEXT, HEAD), jnp.int32),
        v((TAPS, EXT, HEAD), F32),
        v((2, BLK, SPAN), F32),
        v((GROUPS, EXT, PAIR), BF16),
        v((8, 2, BLK, SPAN), F32),
        v((ROWS, WIDTH), BF16),
        v((ROWS, WIDTH), BF16),
        v((NY, 16, HEAD), BF16),
        v((NY, 2, NX, 16, WIDTH), BF16),
        v((GROUPS, PAIR, 512), BF16),
        v((GROUPS, PAIR, 512), F32),
        v((GROUPS, PAIR, 512), BF16),
        v((NZ, NX, 32, 384), BF16),
        v((NX - 1, NZ, 32, 384), BF16),
        v((NZ, NX, 32, 128), BF16),
        v((NZ - 1, NX, 32, 128), BF16),
        v((NZ, 32, 384), BF16),
        v((NZ - 1, 32, 384), BF16),
        v((NX, 32, 128), BF16),
        v((NX - 1, 32, 128), BF16),
        v((NY, 16, HEAD), F32),
        v((NY - 1, 16, HEAD), F32),
        v((16, HEAD), F32),
        v((16, HEAD), F32),
        v((2, WIDTH), F32),
        v((GROUPS, ROWS, PAIR), BF16),
        v((8, EXT, HEAD), F32),
        v((8, EXT, HEAD), F32),
        v((GROUPS, 2, HALF, PAIR), BF16),
        v((GROUPS, 2, FHALO, PAIR), BF16),
        v((GROUPS, 2, HALF, PAIR), BF16),
        v((GROUPS, 2, FHALO, PAIR), BF16),
        v((GROUPS, ROWS, PAIR), BF16),
        v((GROUPS, ROWS, PAIR), BF16),
        v((ROWS, WIDTH), BF16),
        v((2, KROWS, HEAD), F32),
        v((KROWS, HEAD), F32),
        v((NX, KROWS, HEAD), F32),
        v((NZ, KROWS, HEAD), BF16),
        v((NY, KROWS, HEAD), BF16),
        v((2, KROWS, HEAD), F32),
        v((TAPS, WIDTH), F32),
        pltpu.SemaphoreType.DMA((NSEM,)),
        pltpu.SemaphoreType.DMA((NSEM,)),
        pltpu.SemaphoreType.DMA((48,)),
    ]
    shapes = (
        sheet, sheet, sheet, sheet,
        jax.ShapeDtypeStruct((TAPS, WIDTH), F32),
        jax.ShapeDtypeStruct((2, WIDTH), F32),
    )
    results = pl.pallas_call(
        functools.partial(kernel, norm),
        out_shape=shapes,
        in_specs=[any_spec] * 6 + [pl.BlockSpec(memory_space=pltpu.SMEM)],
        out_specs=[any_spec] * 6,
        scratch_shapes=scratch,
        compiler_params=pltpu.CompilerParams(
            collective_id=0, has_side_effects=True, vmem_limit_bytes=56 * 1024 * 1024
        ),
        name="block",
    )(features[0], queries[0], key_rows[0], kernel_taps, out_weight.T, cotangent[0], lengths)
    layer, grad_q, grad_k, grad_in, grad_kernel, grad_weight = pl.pallas_call(
        hand_over,
        out_shape=shapes,
        in_specs=[any_spec] * 6,
        out_specs=[any_spec] * 6,
        scratch_shapes=[v(shape.shape, shape.dtype) for shape in shapes] + [pltpu.SemaphoreType.DMA((12,))],
        name="hand_over",
    )(*results)
    return (layer[None], grad_q[None], grad_k[None], grad_in[None], grad_kernel, grad_weight)


def solution(mesh):
    sheet = P("dp", "seq", None)
    in_specs = (sheet, sheet, sheet, P(), P(None, "seq"), sheet, P("dp", None))
    out_specs = (sheet, sheet, sheet, sheet, P(), P(("dp", "seq"), None))
    return jax.shard_map(body, mesh=mesh, in_specs=in_specs, out_specs=out_specs, check_vma=False)
```

```python
import functools
import math

import jax
import jax.numpy as jnp
from jax import lax
from jax.experimental import pallas as pl
from jax.experimental.pallas import tpu as pltpu
from jax.sharding import PartitionSpec as P

MESH = pl.DeviceIdType.MESH
F32 = jnp.float32
BF16 = jnp.bfloat16

HALF = 128
TAPS = 9
REACH = 4
RIM = 16
UTT = 16
ROWS = 224
WIDTH = 1024
HEAD = 128
PAIR = 256
GROUPS = 4
NX = 4
NZ = 8
NY = 8
EXT = ROWS + 2 * HALF
FEXT = EXT + 2 * RIM
FHALO = HALF + RIM
BLK = 112
SPAN = 384
BLKOFF = 96
NSEM = 160
KROWS = 48


def dot(a, b, contract):
    return lax.dot_general(a, b, ((contract[:1], contract[1:]), ((), ())), preferred_element_type=F32)


def kernel(
    norm,
    feat, qry, key, ker, wgt, cot, lens,
    o_layer, o_gq, o_gk, o_gf, o_gker, o_gw,
    fext, fs, kext, qv, cotv, kerv, segs, taps, bias, vext, probs, mixed, backv,
    w1, wt,
    gsend, gown, gcore, ga, gar, gb, gbr, gza, gzar, gxb, gxbr, gs, gsr, gfin, gsib, gwv,
    dqv, dkx, dvx, dks, dvs, dkr, dvr, dkv, gfv, lay,
    kp, kpr, kx, kz, ky, kfin, kout,
    ss, rs, ls,
):
    dp = lax.axis_index("dp")
    sq = lax.axis_index("seq")
    z, x = dp // NX, dp % NX
    y, c = sq // 2, sq % 2
    nseq = 2 * NY
    seqlen = nseq * ROWS
    offset = sq * ROWS

    def dev(d, s):
        return {"dp": d, "seq": s}

    sib = dev(dp, sq + 1 - 2 * c)
    right = dev(dp, (sq + 1) % nseq)
    left = dev(dp, (sq + nseq - 1) % nseq)

    def y_peer(k):
        return dev(dp, ((y + k) % NY) * 2 + c)

    def z_peer(k):
        return dev(((z + k) % NZ) * NX + x, sq)

    def x_peer(k):
        return dev(z * NX + (x + k) % NX, sq)

    x_order = (1, 3, 2)
    ring_order = (4, 3, 5, 2, 6, 1, 7)

    barrier = pltpu.get_barrier_semaphore()
    friends = [left, right]
    friends += [y_peer(k) for k in range(1, NY)]
    friends += [z_peer(k) for k in range(1, NZ)]
    friends += [x_peer(k) for k in range(1, NX)]
    for friend in friends:
        pl.semaphore_signal(barrier, inc=1, device_id=friend, device_id_type=MESH)

    used = [0, 0]
    sends = []

    def remote(src, dst, device):
        index = used[0]
        used[0] += 1
        copy = pltpu.make_async_remote_copy(
            src_ref=src, dst_ref=dst, send_sem=ss.at[index], recv_sem=rs.at[index],
            device_id=device, device_id_type=MESH,
        )
        copy.start()
        sends.append(copy)
        return copy

    def local(src, dst):
        index = used[1]
        used[1] += 1
        copy = pltpu.make_async_copy(src, dst, ls.at[index])
        copy.start()
        return copy

    def received(copies):
        for copy in copies:
            copy.wait_recv()

    def cols(g):
        return pl.ds(g * PAIR, PAIR)

    zcol = pl.ds(pl.multiple_of(z * HEAD, HEAD), HEAD)
    w_src = wgt.at[pl.ds(pl.multiple_of(x * 16, 16), 16), zcol]
    w_own = local(w_src, w1.at[y])
    far = (x + 2) % NX
    far_src = wgt.at[pl.ds(pl.multiple_of(far * 16, 16), 16), :]
    far_own = local(far_src, wt.at[y, c, far])
    loads = []
    for g in range(GROUPS):
        loads.append([
            local(feat.at[:, cols(g)], fext.at[g, pl.ds(FHALO, ROWS)]),
            local(key.at[:, cols(g)], kext.at[g, pl.ds(HALF, ROWS)]),
            local(qry.at[:, cols(g)], qv.at[g]),
        ])
    ker_in = local(ker, kerv)
    cot_in = local(cot, cotv)

    pl.semaphore_wait(barrier, len(friends))

    w_y = [remote(w_src, w1.at[y], y_peer(k)) for k in ring_order]
    halos = []
    for g in range(GROUPS):
        halos.append([
            remote(feat.at[pl.ds(ROWS - FHALO, FHALO), cols(g)], fext.at[g, pl.ds(0, FHALO)], right),
            remote(feat.at[pl.ds(0, FHALO), cols(g)], fext.at[g, pl.ds(FHALO + ROWS, FHALO)], left),
            remote(key.at[pl.ds(ROWS - HALF, HALF), cols(g)], kext.at[g, pl.ds(0, HALF)], right),
            remote(key.at[pl.ds(0, HALF), cols(g)], kext.at[g, pl.ds(HALF + ROWS, HALF)], left),
        ])

    w_far = [remote(far_src, wt.at[y, c, far], y_peer(k)) for k in ring_order]

    bounds = []
    total = lens[0, 0]
    bounds.append(total)
    for k in range(1, UTT):
        total = total + lens[0, k]
        bounds.append(total)

    def segment(pos):
        seg = jnp.where(pos < 0, -1, 0)
        for bound in bounds:
            seg = seg + jnp.where(pos >= bound, 1, 0)
        return seg

    for r in range(0, FEXT, 64):
        pos = offset - FHALO + r + lax.broadcasted_iota(jnp.int32, (64, HEAD), 0)
        segs[pl.ds(r, 64), :] = segment(pos)
    for r in range(0, EXT, 96):
        center = segs[pl.ds(RIM + r, 96), :]
        for j in range(TAPS):
            near = segs[pl.ds(RIM - REACH + j + r, 96), :]
            taps[j, pl.ds(r, 96), :] = jnp.where(center == near, 1.0, 0.0).astype(F32)
    for b in range(2):
        colpos = offset - HALF + BLKOFF * b + lax.broadcasted_iota(jnp.int32, (8, SPAN), 1)
        seg_col = segment(colpos)[0:1, :]
        seg_row = segs[pl.ds(FHALO + BLK * b, BLK), :]
        seg_row = jnp.concatenate([seg_row] * (SPAN // HEAD), axis=1)
        gap = (
            lax.broadcasted_iota(jnp.int32, (BLK, SPAN), 0) + (BLK * b + HALF - BLKOFF * b)
            - lax.broadcasted_iota(jnp.int32, (BLK, SPAN), 1)
        )
        ok = (seg_row == seg_col) & (gap <= HALF) & (gap >= -HALF)
        bias[b] = jnp.where(ok, 0.0, -jnp.inf).astype(F32)

    w_own.wait()
    received(w_y)
    wt[:, c, x, :, zcol] = w1[...]
    w_z = [remote(w1, wt.at[:, c, x, :, zcol], z_peer(k)) for k in ring_order]

    scale = HEAD ** -0.5
    scale2 = scale * math.log2(math.e)
    sib_cols = pl.ds(pl.multiple_of((1 - c) * 512, 512), 512)
    own_cols = pl.ds(pl.multiple_of(c * 512, 512), 512)

    def forward(g):
        for copy in loads[g]:
            copy.wait()
        received(halos[g])
        for j in range(2):
            lanes = pl.ds(j * HEAD, HEAD)
            h = 2 * g + j
            fs[h] = fext[g, :, lanes].astype(F32)
            kw = kerv[:, pl.ds(h * HEAD, HEAD)]
            for r in range(0, EXT, 96):
                acc = kw[REACH:REACH + 1, :] * fs[h, pl.ds(r + RIM, 96), :]
                for t in range(TAPS):
                    if t != REACH:
                        f = fs[h, pl.ds(r + RIM - REACH + t, 96), :]
                        acc = acc + (f * taps[t, pl.ds(r, 96), :]) * kw[t:t + 1, :]
                vext[g, pl.ds(r, 96), lanes] = acc.astype(BF16)
        for j in range(2):
            lanes = pl.ds(j * HEAD, HEAD)
            h = 2 * g + j
            for b in range(2):
                qb = qv[g, pl.ds(BLK * b, BLK), lanes]
                kb = kext[g, pl.ds(BLKOFF * b, SPAN), lanes]
                s = dot(qb, kb, (1, 1)) * scale2 + bias[b]
                top = jnp.max(s, axis=1, keepdims=True)
                ex = jnp.exp2(s - top)
                p = ex * (1.0 / jnp.sum(ex, axis=1, keepdims=True))
                probs[h, b] = p
                vb = vext[g, pl.ds(BLKOFF * b, SPAN), lanes]
                mixed[pl.ds(BLK * b, BLK), pl.ds(h * HEAD, HEAD)] = dot(p.astype(BF16), vb, (1, 0)).astype(BF16)

    g_core = [None] * GROUPS
    g_xa = []

    def weight_term(g):
        mb = mixed[:, cols(g)]
        gsend[g] = dot(mb, cotv[:, sib_cols], (0, 0)).astype(BF16)
        g_core[g] = remote(gsend.at[g], gcore.at[g], sib)
        gown[g] = dot(mb, cotv[:, own_cols], (0, 0))

    def weight_along_x(g):
        g_core[g].wait_recv()
        for i in range(2):
            half = pl.ds(i * HEAD, HEAD)
            part = (gown[g, half, :] + gcore[g, half, :].astype(F32)).astype(BF16).reshape(NX, 32, 512)
            ga[2 * g + i] = part[:, :, :384]
            gb[2 * g + i] = part[:, :, 384:]
        two = pl.ds(2 * g, 2)
        for k in x_order:
            g_xa.append(remote(ga.at[two, (x + k) % NX], gar.at[k - 1, two], x_peer(k)))

    ker_in.wait()
    forward(0)
    cot_in.wait()
    weight_term(0)

    forward(1)
    weight_term(1)
    weight_along_x(0)

    w_s = []

    def to_sibling(there):
        w_s.append(remote(wt.at[:, c, there], wt.at[:, c, there], sib))

    received(w_z)
    w_x = {k: remote(wt.at[:, c, x], wt.at[:, c, x], x_peer(k)) for k in (1, 3)}
    to_sibling(x)

    forward(2)
    weight_term(2)
    weight_along_x(1)
    forward(3)
    weight_term(3)
    weight_along_x(2)

    weight_along_x(3)
    g_zb = [remote(gb.at[(z + k) % NZ], gbr.at[k - 1], z_peer(k)) for k in ring_order]

    far_own.wait()
    received(w_far)
    to_sibling(far)
    for k in (1, 3):
        w_x[k].wait_recv()
        to_sibling((x + NX - k) % NX)

    received(w_s)
    wide = wt[...].reshape(WIDTH, WIDTH)
    backv[...] = dot(cotv[...], wide, (1, 0)).astype(BF16)

    dv_halos = []
    for g in range(GROUPS):
        for j in range(2):
            lanes = pl.ds(j * HEAD, HEAD)
            h = 2 * g + j
            first, second = [
                dot(probs[h, b].astype(BF16), backv[pl.ds(BLK * b, BLK), pl.ds(h * HEAD, HEAD)], (0, 0)) for b in range(2)
            ]
            dvx[h, pl.ds(0, BLKOFF), :] = first[:BLKOFF]
            dvx[h, pl.ds(BLKOFF, SPAN - BLKOFF), :] = first[BLKOFF:] + second[:SPAN - BLKOFF]
            dvx[h, pl.ds(SPAN, EXT - SPAN), :] = second[SPAN - BLKOFF:]
            sums = [jnp.zeros((8, HEAD), F32) for _ in range(TAPS)]
            for r in range(0, EXT, 96):
                gv = dvx[h, pl.ds(r, 96), :]
                for t in range(TAPS):
                    term = gv * fs[h, pl.ds(r + RIM - REACH + t, 96), :]
                    if t != REACH:
                        term = term * taps[t, pl.ds(r, 96), :]
                    sums[t] = sums[t] + jnp.sum(term.reshape(12, 8, HEAD), axis=0)
            rows = jnp.concatenate([jnp.sum(v, axis=0, keepdims=True) for v in sums], axis=0)
            kp[h // 4, pl.ds((h % 4) * TAPS, TAPS), :] = rows
            dvs[g, 0, :, lanes] = dvx[h, pl.ds(0, FHALO), :].astype(BF16)
            dvs[g, 1, :, lanes] = dvx[h, pl.ds(EXT - FHALO, FHALO), :].astype(BF16)
    k_sib = remote(kp.at[1 - c], kpr, sib)
    for g in range(GROUPS):
        dv_halos.append([
            remote(dvs.at[g, 0], dvr.at[g, 0], left),
            remote(dvs.at[g, 1], dvr.at[g, 1], right),
        ])

    outs = []
    dk_halos = []

    def backward(g):
        for j in range(2):
            lanes = pl.ds(j * HEAD, HEAD)
            h = 2 * g + j
            bh = backv[:, pl.ds(h * HEAD, HEAD)]
            mh = mixed[:, pl.ds(h * HEAD, HEAD)]
            inner = jnp.sum(bh.astype(F32) * mh.astype(F32), axis=1, keepdims=True)
            parts = []
            for b in range(2):
                rows = slice(BLK * b, BLK * b + BLK)
                kb = kext[g, pl.ds(BLKOFF * b, SPAN), lanes]
                vb = vext[g, pl.ds(BLKOFF * b, SPAN), lanes]
                qb = qv[g, pl.ds(BLK * b, BLK), lanes]
                ds = (probs[h, b] * (dot(bh[rows], vb, (1, 1)) - inner[rows])).astype(BF16)
                dqv[g, pl.ds(BLK * b, BLK), lanes] = (dot(ds, kb, (1, 0)) * scale).astype(BF16)
                parts.append(dot(ds, qb, (0, 0)) * scale)
            first, second = parts
            dkx[h, pl.ds(0, BLKOFF), :] = first[:BLKOFF]
            dkx[h, pl.ds(BLKOFF, SPAN - BLKOFF), :] = first[BLKOFF:] + second[:SPAN - BLKOFF]
            dkx[h, pl.ds(SPAN, EXT - SPAN), :] = second[SPAN - BLKOFF:]
            dks[g, 0, :, lanes] = dkx[h, pl.ds(0, HALF), :].astype(BF16)
            dks[g, 1, :, lanes] = dkx[h, pl.ds(EXT - HALF, HALF), :].astype(BF16)
        dk_halos.append([
            remote(dks.at[g, 0], dkr.at[g, 0], left),
            remote(dks.at[g, 1], dkr.at[g, 1], right),
        ])
        outs.append(local(dqv.at[g], o_gq.at[:, cols(g)]))

    def finish(g):
        received(dv_halos[g])
        for j in range(2):
            lanes = pl.ds(j * HEAD, HEAD)
            h = 2 * g + j
            dvx[h, pl.ds(HALF - RIM, FHALO), :] += dvr[g, 1, :, lanes].astype(F32)
            dvx[h, pl.ds(ROWS, FHALO), :] += dvr[g, 0, :, lanes].astype(F32)
            kw = kerv[:, pl.ds(h * HEAD, HEAD)]
            for r in range(0, ROWS, BLK):
                acc = kw[REACH:REACH + 1, :] * dvx[h, pl.ds(HALF + r, BLK), :]
                for t in range(TAPS):
                    if t != REACH:
                        v = dvx[h, pl.ds(HALF + r - t + REACH, BLK), :]
                        acc = acc + (v * taps[TAPS - 1 - t, pl.ds(HALF + r, BLK), :]) * kw[t:t + 1, :]
                gfv[g, pl.ds(r, BLK), lanes] = acc.astype(BF16)
        outs.append(local(gfv.at[g], o_gf.at[:, cols(g)]))
        received(dk_halos[g])
        for j in range(2):
            lanes = pl.ds(j * HEAD, HEAD)
            h = 2 * g + j
            dkx[h, pl.ds(HALF, HALF), :] += dkr[g, 1, :, lanes].astype(F32)
            dkx[h, pl.ds(ROWS, HALF), :] += dkr[g, 0, :, lanes].astype(F32)
            dkv[g, :, lanes] = dkx[h, pl.ds(HALF, ROWS), :].astype(BF16)
        outs.append(local(dkv.at[g], o_gk.at[:, cols(g)]))

    backward(0)
    k_sib.wait_recv()
    kx[x] = kp[c] + kpr[...]
    k_x = [remote(kx.at[x], kx.at[x], x_peer(k)) for k in x_order]

    received(g_xa)
    for i in range(NZ):
        part = ga[i, x].astype(F32)
        for k in range(NX - 1):
            part = part + gar[k, i].astype(F32)
        gza[i] = part.astype(BF16)
    g_za = [remote(gza.at[(z + k) % NZ], gzar.at[k - 1], z_peer(k)) for k in ring_order]
    received(g_zb)
    for i in range(NX):
        part = gb[z, i].astype(F32)
        for k in range(NZ - 1):
            part = part + gbr[k, i].astype(F32)
        gxb[i] = part.astype(BF16)
    g_xb = [remote(gxb.at[(x + k) % NX], gxbr.at[k - 1], x_peer(k)) for k in x_order]

    backward(1)
    received(k_x)
    kz[z] = (kx[0] + kx[1] + kx[2] + kx[3]).astype(BF16)
    k_z = [remote(kz.at[z], kz.at[z], z_peer(k)) for k in ring_order]

    backward(2)
    backward(3)
    finish(0)

    received(k_z)
    part = kz[0].astype(F32)
    for k in range(1, NZ):
        part = part + kz[k].astype(F32)
    ky[y] = part.astype(BF16)
    k_y = [remote(ky.at[y], ky.at[y], y_peer(k)) for k in ring_order]

    finish(1)

    received(g_za)
    received(g_xb)
    part = gza[z].astype(F32)
    for k in range(NZ - 1):
        part = part + gzar[k].astype(F32)
    last = gxb[x].astype(F32)
    for k in range(NX - 1):
        last = last + gxbr[k].astype(F32)
    part = jnp.concatenate([part, last], axis=1)
    for s in range(NY):
        for i in range(4):
            gs[s, pl.ds(4 * i, 4), :] = part[4 * s:4 * s + 4, i * HEAD:(i + 1) * HEAD]
    g_y = [remote(gs.at[(y + k) % NY], gsr.at[k - 1], y_peer(k)) for k in ring_order]

    finish(2)
    finish(3)
    lay[...] = dot(mixed[...], wt[...].reshape(WIDTH, WIDTH), (1, 1)).astype(BF16)
    outs.append(local(lay, o_layer))

    received(k_y)
    part = ky[0].astype(F32)
    for k in range(1, NY):
        part = part + ky[k].astype(F32)
    kfin[c] = part * norm
    k_last = remote(kfin.at[c], kfin.at[c], sib)

    received(g_y)
    part = gs[y]
    for k in range(NY - 1):
        part = part + gsr[k]
    gfin[...] = part * norm
    g_last = remote(gfin, gsib, sib)

    k_last.wait_recv()
    for h in range(8):
        kout[:, h * HEAD:(h + 1) * HEAD] = kfin[h // 4, pl.ds((h % 4) * TAPS, TAPS), :]
    outs.append(local(kout, o_gker))

    g_last.wait_recv()
    mine, theirs = gfin[...], gsib[...]
    low = jnp.where(c == 0, mine, theirs)
    high = jnp.where(c == 0, theirs, mine)
    for n, half in enumerate((low, high)):
        for i in range(4):
            rows = jnp.where(c == 0, half[4 * i:4 * i + 2, :], half[4 * i + 2:4 * i + 4, :])
            gwv[:, n * 512 + i * HEAD:n * 512 + (i + 1) * HEAD] = rows
    outs.append(local(gwv, o_gw))

    for copy in outs:
        copy.wait()
    for copy in sends:
        copy.wait_send()


def hand_over(*refs):
    given, out, held, sem = refs[:6], refs[6:12], refs[12:18], refs[18]
    loads = [pltpu.make_async_copy(given[i], held[i], sem.at[i]) for i in range(6)]
    stores = [pltpu.make_async_copy(held[i], out[i], sem.at[6 + i]) for i in range(6)]
    for copy in loads:
        copy.start()
    for load, store in zip(loads, stores):
        load.wait()
        store.start()
    for copy in stores:
        copy.wait()


def body(features, queries, key_rows, kernel_taps, out_weight, cotangent, lengths):
    norm = float(lax.axis_size("dp") * lax.axis_size("seq") * ROWS) ** -0.5
    any_spec = pl.BlockSpec(memory_space=pl.ANY)
    sheet = jax.ShapeDtypeStruct((ROWS, WIDTH), BF16)
    v = pltpu.VMEM
    scratch = [
        v((GROUPS, FEXT, PAIR), BF16),
        v((8, FEXT, HEAD), F32),
        v((GROUPS, EXT, PAIR), BF16),
        v((GROUPS, ROWS, PAIR), BF16),
        v((ROWS, WIDTH), BF16),
        v((TAPS, WIDTH), F32),
        v((FEXT, HEAD), jnp.int32),
        v((TAPS, EXT, HEAD), F32),
        v((2, BLK, SPAN), F32),
        v((GROUPS, EXT, PAIR), BF16),
        v((8, 2, BLK, SPAN), F32),
        v((ROWS, WIDTH), BF16),
        v((ROWS, WIDTH), BF16),
        v((NY, 16, HEAD), BF16),
        v((NY, 2, NX, 16, WIDTH), BF16),
        v((GROUPS, PAIR, 512), BF16),
        v((GROUPS, PAIR, 512), F32),
        v((GROUPS, PAIR, 512), BF16),
        v((NZ, NX, 32, 384), BF16),
        v((NX - 1, NZ, 32, 384), BF16),
        v((NZ, NX, 32, 128), BF16),
        v((NZ - 1, NX, 32, 128), BF16),
        v((NZ, 32, 384), BF16),
        v((NZ - 1, 32, 384), BF16),
        v((NX, 32, 128), BF16),
        v((NX - 1, 32, 128), BF16),
        v((NY, 16, HEAD), F32),
        v((NY - 1, 16, HEAD), F32),
        v((16, HEAD), F32),
        v((16, HEAD), F32),
        v((2, WIDTH), F32),
        v((GROUPS, ROWS, PAIR), BF16),
        v((8, EXT, HEAD), F32),
        v((8, EXT, HEAD), F32),
        v((GROUPS, 2, HALF, PAIR), BF16),
        v((GROUPS, 2, FHALO, PAIR), BF16),
        v((GROUPS, 2, HALF, PAIR), BF16),
        v((GROUPS, 2, FHALO, PAIR), BF16),
        v((GROUPS, ROWS, PAIR), BF16),
        v((GROUPS, ROWS, PAIR), BF16),
        v((ROWS, WIDTH), BF16),
        v((2, KROWS, HEAD), F32),
        v((KROWS, HEAD), F32),
        v((NX, KROWS, HEAD), F32),
        v((NZ, KROWS, HEAD), BF16),
        v((NY, KROWS, HEAD), BF16),
        v((2, KROWS, HEAD), F32),
        v((TAPS, WIDTH), F32),
        pltpu.SemaphoreType.DMA((NSEM,)),
        pltpu.SemaphoreType.DMA((NSEM,)),
        pltpu.SemaphoreType.DMA((48,)),
    ]
    shapes = (
        sheet, sheet, sheet, sheet,
        jax.ShapeDtypeStruct((TAPS, WIDTH), F32),
        jax.ShapeDtypeStruct((2, WIDTH), F32),
    )
    results = pl.pallas_call(
        functools.partial(kernel, norm),
        out_shape=shapes,
        in_specs=[any_spec] * 6 + [pl.BlockSpec(memory_space=pltpu.SMEM)],
        out_specs=[any_spec] * 6,
        scratch_shapes=scratch,
        compiler_params=pltpu.CompilerParams(
            collective_id=0, has_side_effects=True, vmem_limit_bytes=56 * 1024 * 1024
        ),
        name="block",
    )(features[0], queries[0], key_rows[0], kernel_taps, out_weight.T, cotangent[0], lengths)
    layer, grad_q, grad_k, grad_in, grad_kernel, grad_weight = pl.pallas_call(
        hand_over,
        out_shape=shapes,
        in_specs=[any_spec] * 6,
        out_specs=[any_spec] * 6,
        scratch_shapes=[v(shape.shape, shape.dtype) for shape in shapes] + [pltpu.SemaphoreType.DMA((12,))],
        name="hand_over",
    )(*results)
    return (layer[None], grad_q[None], grad_k[None], grad_in[None], grad_kernel, grad_weight)


def solution(mesh):
    sheet = P("dp", "seq", None)
    in_specs = (sheet, sheet, sheet, P(), P(None, "seq"), sheet, P("dp", None))
    out_specs = (sheet, sheet, sheet, sheet, P(), P(("dp", "seq"), None))
    return jax.shard_map(body, mesh=mesh, in_specs=in_specs, out_specs=out_specs, check_vma=False)
```
